32 devices in a mesh: groups: 2 (over y), ctx: 16 (over z, x, core).
Axes of the slice: x: 2, y: 2, z: 4, core: 2. Of those that a mesh axis runs over, the one named last changes fastest.
Arguments:
- queries: bfloat16 [8192, 8192], P(('groups', 'ctx')), parts along dimension 0, may hold values from -10 to 10
- keys: bfloat16 [8192, 1024], P(('groups', 'ctx')), parts along dimension 0, may hold values from -6 to 6
- values: bfloat16 [8192, 1024], P(('groups', 'ctx')), parts along dimension 0, may hold values from -6 to 6
- positions: int32 [8192], P(('groups', 'ctx')), parts along dimension 0, may hold values from 0 to 4096, as said below
- picks: int32 [64, 8, 2], P(('groups', 'ctx')), parts along dimension 0, may hold values from -1 to 31, as said below
Outputs:
- attended: bfloat16 [8192, 8192], P(('groups', 'ctx')), parts along dimension 0
The draws below stay inside these ranges and needn't reach their ends.
There are 2 independent parts, one for each index of `groups`. The reference program is written for one: setup_inputs(seed, part) draws one part's arguments, and reference() takes and returns one part's arrays. A program takes and returns all parts, laid end to end along the dimension named above; each array names one. Nothing has to cross between parts.
Inputs may be any that keep to these rules, and one draw needn't show every extreme that they name: positions never fall from one token to the next and each lies in [index, index + 1]; the first is 0 and the last is 4096. A pick of query block b is -1 or a block held by an earlier shard, so its index is below (b // 2) * 2; it may lie inside the band, and then its keys count twice; the two picks of one query block and head differ when both are set, and both are set or both -1; over the 2 query blocks of one shard and all heads, at most 2 picks name blocks of one shard, and some shard has exactly 2 for some other shard in every draw.
All inputs are finite; a program needn't handle non-finite values.
Results may differ from the reference program's by a relative error of at most 0.009.
Values may be sent and summed in bfloat16 or wider, within the bound.
A program may use at most 192 MiB of HBM per device.

```python
import jax
import jax.numpy as jnp
from jax import lax

QUERY_HEADS = 64
KEY_VALUE_HEADS = 8
HEAD_SIZE = 128
BLOCK_TOKENS = 128
LOCAL_BAND_SIZE = 4
PICKED_BLOCKS = 2
SHARD_BLOCKS = 2
SEQUENCE_BLOCKS = 32
SEQUENCE_TOKENS = 4096
CAP = 2


def draw_keys(key, part):
    rotary_base = jnp.clip(jax.random.normal(jax.random.fold_in(key, 11), (SEQUENCE_TOKENS, KEY_VALUE_HEADS, HEAD_SIZE), jnp.float32), -6.0, 6.0)
    return rotary_base.reshape(SEQUENCE_TOKENS, KEY_VALUE_HEADS * HEAD_SIZE).astype(jnp.bfloat16)


def draw_queries(key, part):
    rotary_base = jnp.clip(jax.random.normal(jax.random.fold_in(key, 12), (SEQUENCE_TOKENS, QUERY_HEADS, HEAD_SIZE), jnp.float32), -6.0, 6.0)
    return rotary_base.reshape(SEQUENCE_TOKENS, QUERY_HEADS * HEAD_SIZE).astype(jnp.bfloat16)


def draw_positions(key, part):
    extra = jax.random.randint(jax.random.fold_in(key, 31), (SEQUENCE_TOKENS,), 0, 2)
    index_value = jnp.arange(SEQUENCE_TOKENS)
    extra = jnp.where(index_value == 0, 0, jnp.where(index_value == SEQUENCE_TOKENS - 1, 1, extra))
    return (index_value + extra).astype(jnp.int32)


def draw_picks(key, part):
    shard_count = SEQUENCE_BLOCKS // SHARD_BLOCKS
    window_length = SHARD_BLOCKS * KEY_VALUE_HEADS
    slots = shard_count * CAP
    needed = 2 * window_length

    def single_shard(shard):
        shard_key = jax.random.fold_in(key, shard)
        last_owner = shard - 1
        is_final = shard == shard_count - 1
        slot_owner = jnp.arange(slots) // CAP
        eligible = slot_owner <= last_owner
        count = jnp.sum(eligible.astype(jnp.int32))
        noise = jax.random.randint(jax.random.fold_in(shard_key, 1), (slots,), 0, 1 << 20)
        score = noise * slots + jnp.arange(slots) + jnp.where(eligible, 0, 1 << 30)
        favored = (slot_owner == last_owner) | is_final & (slot_owner == 0)
        score = jnp.where(favored & eligible, jnp.arange(slots) - slots, score)
        order = jnp.argsort(score).astype(jnp.int32)
        filler = jnp.zeros((max(0, needed - slots),), jnp.int32)
        taken = jnp.concatenate([order, filler])[:needed]
        owners = slot_owner[taken].reshape(window_length, 2)
        live = 2 * jnp.arange(window_length) + 1 < count
        local_first = jax.random.randint(jax.random.fold_in(shard_key, 5), (window_length,), 0, SHARD_BLOCKS)
        local_first = jnp.where(is_final & (owners[:, 0] == 0), SHARD_BLOCKS - 1, local_first)
        stride = jax.random.randint(jax.random.fold_in(shard_key, 6), (window_length,), 1, SHARD_BLOCKS)
        other = jax.random.randint(jax.random.fold_in(shard_key, 7), (window_length,), 0, SHARD_BLOCKS)
        other = jnp.where(is_final & (owners[:, 1] == 0), SHARD_BLOCKS - 1, other)
        local_second = jnp.where(owners[:, 1] == owners[:, 0], (local_first + stride) % SHARD_BLOCKS, other)
        first_choice = jnp.where(live, owners[:, 0] * SHARD_BLOCKS + local_first, -1)
        second_choice = jnp.where(live, owners[:, 1] * SHARD_BLOCKS + local_second, -1)
        return jnp.stack([first_choice, second_choice], -1).reshape(SHARD_BLOCKS, KEY_VALUE_HEADS, 2)
    return jax.vmap(single_shard)(jnp.arange(shard_count)).reshape(SEQUENCE_BLOCKS, KEY_VALUE_HEADS, 2).astype(jnp.int32)


def levels(key, shape, shards, least, top_value):
    loudness = 1.0
    for axis_at, shards_of in shards:
        steps = jax.random.uniform(jax.random.fold_in(jax.random.fold_in(key, 6), axis_at), (shards_of,), jnp.float32, least / len(shards), top_value / len(shards))
        loudness = loudness * jnp.repeat(jnp.exp(steps), shape[axis_at] // shards_of).reshape((-1,) + (1,) * (len(shape) - 1 - axis_at))
    return loudness


def scatter_about(key, dims, spread, most, pieces=(), held_as=jnp.bfloat16):
    values = jax.random.normal(key, dims, jnp.float32) * spread
    if len(pieces) > 0:
        values = levels(key, dims, pieces, -0.22, 0.18) * values
    return jnp.clip(values, min=-most, max=most).astype(held_as)


def setup_inputs(seed: int = 0, part: int = 0) -> dict:
    streams_of = jax.random.split(jax.random.key(seed), 6)
    own_keys = jax.random.split(jax.random.fold_in(streams_of[5], part), 6)
    queries = draw_queries(jax.random.fold_in(jax.random.fold_in(streams_of[5], part), 71), part)
    keys = draw_keys(jax.random.fold_in(jax.random.fold_in(streams_of[5], part), 71), part)
    values = scatter_about(own_keys[2], (SEQUENCE_TOKENS, KEY_VALUE_HEADS * HEAD_SIZE), 1.0, 6.0, ((0, 16),))
    positions = draw_positions(jax.random.fold_in(jax.random.fold_in(streams_of[5], part), 71), part)
    picks = draw_picks(jax.random.fold_in(jax.random.fold_in(streams_of[5], part), 71), part)
    return dict(queries=queries, keys=keys, values=values, positions=positions, picks=picks)


rope_base = 500000.0
masked_score = -1e30


def apply_rotary(x, pos):
    half = x.shape[-1] // 2
    freq = rope_base ** (-(jnp.arange(half, dtype=jnp.float32) * 2.0) / x.shape[-1])
    angle = pos.astype(jnp.float32)[:, None] * freq[None, :]
    cosine = jnp.cos(angle)[:, None, :]
    sine = jnp.sin(angle)[:, None, :]
    wide = x.astype(jnp.float32)
    first_choice = wide[..., :half]
    second_choice = wide[..., half:]
    return jnp.concatenate([first_choice * cosine - second_choice * sine, second_choice * cosine + first_choice * sine], -1).astype(jnp.bfloat16)


def reference(queries, keys, values, positions, picks):
    query_group = QUERY_HEADS // KEY_VALUE_HEADS
    score_scale = HEAD_SIZE ** -0.5
    query_rotated = apply_rotary(queries.reshape(SEQUENCE_TOKENS, QUERY_HEADS, HEAD_SIZE), positions)
    key_rotated = apply_rotary(keys.reshape(SEQUENCE_TOKENS, KEY_VALUE_HEADS, HEAD_SIZE), positions)
    stacked_blocks = jnp.stack([key_rotated, values.reshape(SEQUENCE_TOKENS, KEY_VALUE_HEADS, HEAD_SIZE)], axis=2)
    padded_input = jnp.concatenate([jnp.zeros(((LOCAL_BAND_SIZE - 1) * BLOCK_TOKENS, KEY_VALUE_HEADS, 2, HEAD_SIZE), jnp.bfloat16), stacked_blocks], 0)
    head_numbers = jnp.arange(KEY_VALUE_HEADS, dtype=jnp.int32)
    offsets = jnp.arange(BLOCK_TOKENS, dtype=jnp.int32)

    def one_block(block_number):
        query_block_index = lax.dynamic_slice_in_dim(query_rotated, block_number * BLOCK_TOKENS, BLOCK_TOKENS, 0).reshape(BLOCK_TOKENS, KEY_VALUE_HEADS, query_group, HEAD_SIZE).astype(jnp.float32)
        local_window = lax.dynamic_slice_in_dim(padded_input, block_number * BLOCK_TOKENS, LOCAL_BAND_SIZE * BLOCK_TOKENS, 0).astype(jnp.float32)
        chosen = lax.dynamic_index_in_dim(picks, block_number, 0, keepdims=False)
        start = jnp.maximum(chosen, 0).astype(jnp.int32) * BLOCK_TOKENS
        token_ids = (start[:, :, None] + offsets[None, None, :]).astype(jnp.int32)
        foreign_blocks = stacked_blocks[token_ids, head_numbers[:, None, None]].astype(jnp.float32)
        near_scores = jnp.einsum('qhgd,khd->hgqk', query_block_index, local_window[:, :, 0]) * score_scale
        distant_scores = jnp.einsum('font,ouyt->onfuy', query_block_index, foreign_blocks[:, :, :, 0]).reshape(KEY_VALUE_HEADS, query_group, BLOCK_TOKENS, PICKED_BLOCKS * BLOCK_TOKENS) * score_scale
        key_tok = (block_number - (LOCAL_BAND_SIZE - 1)) * BLOCK_TOKENS + jnp.arange(LOCAL_BAND_SIZE * BLOCK_TOKENS, dtype=jnp.int32)
        query_tok = block_number * BLOCK_TOKENS + offsets
        near_mask = (key_tok[None, :] >= 0) & (key_tok[None, :] <= query_tok[:, None])
        far_mask = jnp.repeat(chosen >= 0, BLOCK_TOKENS, axis=1)[:, None, None, :]
        near_scores = jnp.where(near_mask, near_scores, masked_score)
        distant_scores = jnp.where(far_mask, distant_scores, masked_score)
        top = jnp.maximum(jnp.max(near_scores, -1), jnp.max(distant_scores, -1))[..., None]
        near_exp = jnp.exp(near_scores - top)
        distant_exponent = jnp.exp(distant_scores - top)
        total = jnp.sum(near_exp, -1) + jnp.sum(distant_exponent, -1)
        near_w = lax.optimization_barrier(near_exp.astype(jnp.bfloat16)).astype(jnp.float32)
        distant_weight = lax.optimization_barrier(distant_exponent.astype(jnp.bfloat16)).astype(jnp.float32)
        distant_weight = distant_weight.reshape(KEY_VALUE_HEADS, query_group, BLOCK_TOKENS, PICKED_BLOCKS, BLOCK_TOKENS)
        summed = jnp.einsum('hgqk,khd->qhgd', near_w, local_window[:, :, 1]) + jnp.einsum('hgqpk,hpkd->qhgd', distant_weight, foreign_blocks[:, :, :, 1])
        result = summed / jnp.transpose(total, (2, 0, 1))[..., None]
        return result.reshape(BLOCK_TOKENS, QUERY_HEADS * HEAD_SIZE).astype(jnp.bfloat16)

    blocks = lax.map(one_block, jnp.arange(SEQUENCE_BLOCKS, dtype=jnp.int32))
    return blocks.reshape(SEQUENCE_TOKENS, QUERY_HEADS * HEAD_SIZE)
```

```python
import functools

import jax
import jax.numpy as jnp
from jax import lax
from jax.experimental import pallas as pl
from jax.experimental.pallas import tpu as pltpu
from jax.sharding import PartitionSpec as P

QUERY_HEADS = 64
KEY_VALUE_HEADS = 8
HEAD_SIZE = 128
BLOCK_TOKENS = 128
LOCAL_BAND_SIZE = 4
PICKED_BLOCKS = 2
GROUP = QUERY_HEADS // KEY_VALUE_HEADS

rope_base = 500000.0
masked_score = -1e30
log2_e = 1.4426950408889634


def from_behind(block, axis, distance):
    devices = range(lax.axis_size(axis))
    route = [(i - distance, i) for i in devices if i - distance in devices]
    return lax.ppermute(block, axis, route)


def rotate(x, cosine, sine):
    wide = x.astype(jnp.float32)
    return wide * cosine + pltpu.roll(wide, HEAD_SIZE // 2, 1) * sine


def kv_kernel(keys, values, cosine, sine, kv):
    for head in range(KEY_VALUE_HEADS):
        columns = slice(head * HEAD_SIZE, (head + 1) * HEAD_SIZE)
        kv[0, head, 0] = rotate(keys[:, columns], cosine[...], sine[...]).astype(jnp.bfloat16)
        kv[0, head, 1] = values[:, columns]


def dot_nt(a, b):
    return lax.dot_general(a, b, (((1,), (1,)), ((), ())), preferred_element_type=jnp.float32)


def with_ones(v):
    return jnp.concatenate([v, jnp.ones_like(v)], 1)


def band_kernel(blocks, me, queries, cosine, sine, far, near, own, rotated, partial, stats):
    k_all = jnp.concatenate([far[0, 0]] + [near[i, 0, 0] for i in range(blocks)] + [own[i, 0, 0] for i in range(blocks)], 0)
    v_all = with_ones(
        jnp.concatenate([far[0, 1]] + [near[i, 0, 1] for i in range(blocks)] + [own[i, 0, 1] for i in range(blocks)], 0)
    )
    width = LOCAL_BAND_SIZE * BLOCK_TOKENS
    row = lax.broadcasted_iota(jnp.int32, (BLOCK_TOKENS, width), 0)
    column = lax.broadcasted_iota(jnp.int32, (BLOCK_TOKENS, width), 1)
    lane = lax.broadcasted_iota(jnp.int32, (BLOCK_TOKENS, 128), 1)
    for i in range(blocks):
        first = (me[0] * blocks + i - (LOCAL_BAND_SIZE - 1)) * BLOCK_TOKENS
        good = (column <= row + (LOCAL_BAND_SIZE - 1) * BLOCK_TOKENS) & (column + first >= 0)
        bias = jnp.where(good, 0.0, masked_score)
        k = k_all[i * BLOCK_TOKENS : i * BLOCK_TOKENS + width]
        v = v_all[i * BLOCK_TOKENS : i * BLOCK_TOKENS + width]
        rows = slice(i * BLOCK_TOKENS, (i + 1) * BLOCK_TOKENS)
        held = jnp.zeros((BLOCK_TOKENS, 128), jnp.float32)
        for n in range(GROUP):
            columns = slice(n * HEAD_SIZE, (n + 1) * HEAD_SIZE)
            q = rotate(queries[rows, columns], cosine[rows], sine[rows]).astype(jnp.bfloat16)
            rotated[rows, columns] = q
            score = dot_nt(q, k) + bias
            top = jnp.max(score, 1, keepdims=True)
            weight = jnp.exp2(score - top).astype(jnp.bfloat16)
            summed = jnp.dot(weight, v, preferred_element_type=jnp.float32)
            total = summed[:, HEAD_SIZE:]
            partial[rows, columns] = (summed[:, :HEAD_SIZE] / total).astype(jnp.bfloat16)
            held = jnp.where(lane == n, top + jnp.log2(total), held)
        stats[0, rows] = held


def pick_kernel(blocks, slots, live, rotated, partial, stats, *rest):
    landed, out = rest[:-1], rest[-1]
    head = pl.program_id(0)
    column = lax.broadcasted_iota(jnp.int32, (1, PICKED_BLOCKS * BLOCK_TOKENS), 1)
    for i in range(blocks):
        pair = landed[i * PICKED_BLOCKS : (i + 1) * PICKED_BLOCKS]
        k = jnp.concatenate([p[0, 0] for p in pair], 0)
        v = with_ones(jnp.concatenate([p[0, 1] for p in pair], 0))
        bias = jnp.zeros(column.shape, jnp.float32)
        for p in range(PICKED_BLOCKS):
            at = (i * KEY_VALUE_HEADS + head) * PICKED_BLOCKS + p
            gone = jnp.where(live[at] > 0, 0.0, masked_score)
            bias = jnp.where(column // BLOCK_TOKENS == p, gone, bias)
        rows = slice(i * BLOCK_TOKENS, (i + 1) * BLOCK_TOKENS)
        for n in range(GROUP):
            columns = slice(n * HEAD_SIZE, (n + 1) * HEAD_SIZE)
            score = dot_nt(rotated[rows, columns], k) + bias
            near_top = stats[0, rows, n : n + 1]
            top = jnp.maximum(jnp.max(score, 1, keepdims=True), near_top)
            weight = jnp.exp2(score - top).astype(jnp.bfloat16)
            summed = jnp.dot(weight, v, preferred_element_type=jnp.float32)
            near_weight = jnp.exp2(near_top - top)
            result = (partial[rows, columns].astype(jnp.float32) * near_weight + summed[:, :HEAD_SIZE]) / (
                near_weight + summed[:, HEAD_SIZE:]
            )
            out[rows, columns] = result.astype(jnp.bfloat16)


def shards(queries, keys, values, positions, picks):
    tokens = queries.shape[0]
    blocks = tokens // BLOCK_TOKENS
    window = lax.axis_size("ctx")
    me = lax.axis_index("ctx")
    cap = max(1, blocks * KEY_VALUE_HEADS * PICKED_BLOCKS // window)
    entry_dims = (2, BLOCK_TOKENS, HEAD_SIZE)
    per_head = GROUP * HEAD_SIZE

    half = HEAD_SIZE // 2
    freq = rope_base ** (-(jnp.arange(half, dtype=jnp.float32) * 2.0) / HEAD_SIZE)
    angle = positions.astype(jnp.float32)[:, None] * freq[None, :]
    cosine, sine = jnp.cos(angle), jnp.sin(angle)
    cosine = jnp.concatenate([cosine, cosine], 1)
    sine = jnp.concatenate([-sine, sine], 1)
    factor = HEAD_SIZE**-0.5 * log2_e

    row_spec = pl.BlockSpec((BLOCK_TOKENS, KEY_VALUE_HEADS * HEAD_SIZE), lambda i: (i, 0))
    angle_spec = pl.BlockSpec((BLOCK_TOKENS, HEAD_SIZE), lambda i: (i, 0))
    kv = pl.pallas_call(
        kv_kernel,
        grid=(blocks,),
        in_specs=[row_spec, row_spec, angle_spec, angle_spec],
        out_specs=pl.BlockSpec((1, KEY_VALUE_HEADS) + entry_dims, lambda i: (i, 0, 0, 0, 0)),
        out_shape=jax.ShapeDtypeStruct((blocks, KEY_VALUE_HEADS) + entry_dims, jnp.bfloat16),
        name="rotate_keys",
    )(keys, values, cosine, sine)

    near = from_behind(kv, "ctx", 1)
    far = from_behind(kv[blocks - 1], "ctx", 2)

    flat = picks.reshape(-1)
    count = flat.shape[0]
    live = flat >= 0
    index = jnp.maximum(flat, 0)
    owner = index // blocks
    order = jnp.arange(count, dtype=jnp.int32)
    entry = index % blocks * KEY_VALUE_HEADS + order // PICKED_BLOCKS % KEY_VALUE_HEADS
    same = live[:, None] & live[None, :] & (owner[:, None] == owner[None, :]) & (order[None, :] < order[:, None])
    rank = jnp.sum(same.astype(jnp.int32), axis=1)
    target = owner * cap + rank
    slot_ids = jnp.arange(window * cap, dtype=jnp.int32)
    hits = (target[:, None] == slot_ids[None, :]) & live[:, None]
    table = jnp.sum(jnp.where(hits, entry[:, None], 0), axis=0).reshape(window, cap)
    wanted = lax.all_to_all(table, "ctx", split_axis=0, concat_axis=0, tiled=True)
    answers = kv.reshape((blocks * KEY_VALUE_HEADS,) + entry_dims)[wanted.reshape(-1)]
    landed = lax.all_to_all(answers, "ctx", split_axis=0, concat_axis=0, tiled=True)
    slots = owner * cap + jnp.minimum(rank, cap - 1)

    all_rows = pl.BlockSpec((tokens, HEAD_SIZE), lambda h: (0, 0))
    head_columns = pl.BlockSpec((tokens, per_head), lambda h: (0, h))
    head_blocks = pl.BlockSpec((blocks, 1) + entry_dims, lambda h: (0, h, 0, 0, 0))
    stats_spec = pl.BlockSpec((1, tokens, 128), lambda h: (h, 0, 0))
    limit = pltpu.CompilerParams(vmem_limit_bytes=32 * 1024 * 1024)
    width = LOCAL_BAND_SIZE * BLOCK_TOKENS
    rotated, partial, stats = pl.pallas_call(
        functools.partial(band_kernel, blocks),
        grid=(KEY_VALUE_HEADS,),
        in_specs=[
            pl.BlockSpec(memory_space=pltpu.SMEM),
            head_columns,
            all_rows,
            all_rows,
            pl.BlockSpec((1,) + entry_dims, lambda h: (h, 0, 0, 0)),
            head_blocks,
            head_blocks,
        ],
        out_specs=[head_columns, head_columns, stats_spec],
        out_shape=[
            jax.ShapeDtypeStruct(queries.shape, jnp.bfloat16),
            jax.ShapeDtypeStruct(queries.shape, jnp.bfloat16),
            jax.ShapeDtypeStruct((KEY_VALUE_HEADS, tokens, 128), jnp.float32),
        ],
        compiler_params=limit,
        cost_estimate=pl.CostEstimate(
            flops=4 * tokens * QUERY_HEADS * HEAD_SIZE * width * 2,
            bytes_accessed=tokens * QUERY_HEADS * HEAD_SIZE * 6,
            transcendentals=tokens * QUERY_HEADS * width,
        ),
        name="band_attention",
    )(me.reshape(1), queries, cosine * factor, sine * factor, far, near, kv)

    def slot_spec(i, p):
        def place(h, slot, alive):
            return (slot[(i * KEY_VALUE_HEADS + h) * PICKED_BLOCKS + p], 0, 0, 0)

        return pl.BlockSpec((1,) + entry_dims, place)

    head_columns = pl.BlockSpec((tokens, per_head), lambda h, *_: (0, h))
    return pl.pallas_call(
        functools.partial(pick_kernel, blocks),
        grid_spec=pltpu.PrefetchScalarGridSpec(
            num_scalar_prefetch=2,
            grid=(KEY_VALUE_HEADS,),
            in_specs=[head_columns, head_columns, pl.BlockSpec((1, tokens, 128), lambda h, *_: (h, 0, 0))]
            + [slot_spec(i, p) for i in range(blocks) for p in range(PICKED_BLOCKS)],
            out_specs=head_columns,
        ),
        out_shape=jax.ShapeDtypeStruct(queries.shape, jnp.bfloat16),
        compiler_params=limit,
        name="picked_attention",
    )(slots, live.astype(jnp.int32), rotated, partial, stats, *[landed] * (blocks * PICKED_BLOCKS))


def solution(mesh):
    rows = P(("groups", "ctx"), None)
    return jax.shard_map(
        shards,
        mesh=mesh,
        in_specs=(rows, rows, rows, P(("groups", "ctx")), P(("groups", "ctx"), None, None)),
        out_specs=rows,
        check_vma=False,
    )
```

```python
import functools

import jax
import jax.numpy as jnp
from jax import lax
from jax.experimental import pallas as pl
from jax.experimental.pallas import tpu as pltpu
from jax.sharding import PartitionSpec as P

QUERY_HEADS = 64
KEY_VALUE_HEADS = 8
HEAD_SIZE = 128
BLOCK_TOKENS = 128
LOCAL_BAND_SIZE = 4
PICKED_BLOCKS = 2
GROUP = QUERY_HEADS // KEY_VALUE_HEADS
ENTRY = (2, BLOCK_TOKENS, HEAD_SIZE)

rope_base = 500000.0
masked_score = -1e30
log2_e = 1.4426950408889634


def rotate(x, cosine, sine):
    wide = x.astype(jnp.float32)
    return wide * cosine + pltpu.roll(wide, HEAD_SIZE // 2, 1) * sine


def dot_nt(a, b):
    return lax.dot_general(a, b, (((1,), (1,)), ((), ())), preferred_element_type=jnp.float32)


def with_ones(v):
    return jnp.concatenate([v, jnp.ones_like(v)], 1)


def stack_heads(x):
    return jnp.concatenate([x[:, n * HEAD_SIZE : (n + 1) * HEAD_SIZE] for n in range(GROUP)], 0)


def head_rows(n):
    return slice(n * BLOCK_TOKENS, (n + 1) * BLOCK_TOKENS)


def flip(a, b, size):
    out, bit = 0, 1
    while bit < size:
        out = out + (a // bit + b // bit) % 2 * bit
        bit *= 2
    return out


def exchange_kernel(
    blocks, window, cap,
    queries, keys, values, cosine, sine, pick_row, pick_column,
    rotated, partial, stats, landed, slots,
    q_held, rotated_held, partial_held, stats_held, kv, near, far, answers, request, requests, scalars,
    load_sem, store_sem, near_sem, far_sem, request_send, request_recv, scalar_sem, answer_send, answer_recv,
):
    me = lax.axis_index("ctx")
    count = pick_row.shape[1]
    per_head = GROUP * HEAD_SIZE
    barrier = pltpu.get_barrier_semaphore()

    def greet(j, carry):
        pl.semaphore_signal(barrier, inc=1, device_id={"ctx": lax.rem(me + j, window)})
        return carry

    lax.fori_loop(1, window, greet, 0)

    def load(h):
        columns = pl.ds(pl.multiple_of(h * per_head, per_head), per_head)
        return pltpu.make_async_copy(queries.at[:, columns], q_held.at[h], load_sem.at[h])

    def start_load(h, carry):
        load(h).start()
        return carry

    lax.fori_loop(0, KEY_VALUE_HEADS, start_load, 0)

    row, column = pick_row[...], pick_column[...]
    row_owner = jnp.maximum(row, 0) // blocks
    column_owner = jnp.maximum(column, 0) // blocks
    first = lax.broadcasted_iota(jnp.int32, (count, count), 0)
    second = lax.broadcasted_iota(jnp.int32, (count, count), 1)
    alike = (column_owner == row_owner) & (column >= 0) & (row >= 0)
    column_rank = jnp.sum((alike & (second < first)).astype(jnp.int32), 1, keepdims=True)
    row_rank = jnp.sum((alike & (first < second)).astype(jnp.int32), 0, keepdims=True)
    slots[...] = jnp.where(row >= 0, row_owner * cap + jnp.minimum(row_rank, cap - 1), -1)
    order = lax.broadcasted_iota(jnp.int32, (count, 1), 0)
    entry = jnp.maximum(column, 0) % blocks * KEY_VALUE_HEADS + order // PICKED_BLOCKS % KEY_VALUE_HEADS
    lane = lax.broadcasted_iota(jnp.int32, (count, request.shape[1]), 1)
    hit = (column_owner * cap + column_rank == lane) & (column >= 0)
    request[...] = jnp.sum(jnp.where(hit, entry, 0), 0, keepdims=True)

    for i in range(blocks):
        rows = slice(i * BLOCK_TOKENS, (i + 1) * BLOCK_TOKENS)
        for head in range(KEY_VALUE_HEADS):
            columns = slice(head * HEAD_SIZE, (head + 1) * HEAD_SIZE)
            kv[i * KEY_VALUE_HEADS + head, 0] = rotate(keys[rows, columns], cosine[rows], sine[rows]).astype(jnp.bfloat16)
            kv[i * KEY_VALUE_HEADS + head, 1] = values[rows, columns]

    @pl.when(me < 1)
    def _():
        near[...] = jnp.zeros_like(near)

    @pl.when(me < 2)
    def _():
        far[...] = jnp.zeros_like(far)

    pl.semaphore_wait(barrier, window - 1)

    def ask(owner):
        return pltpu.make_async_remote_copy(
            src_ref=request, dst_ref=requests.at[me], send_sem=request_send.at[owner], recv_sem=request_recv.at[me],
            device_id={"ctx": owner},
        )

    def asked(source):
        return pltpu.make_async_remote_copy(
            src_ref=request, dst_ref=requests.at[source], send_sem=request_send.at[source],
            recv_sem=request_recv.at[source], device_id={"ctx": source},
        )

    def start_ask(owner, carry):
        ask(owner).start()
        return carry

    lax.fori_loop(0, me, start_ask, 0)

    last = pl.ds((blocks - 1) * KEY_VALUE_HEADS, KEY_VALUE_HEADS)
    send_near = pltpu.make_async_remote_copy(
        src_ref=kv, dst_ref=near, send_sem=near_sem.at[0], recv_sem=near_sem.at[1],
        device_id={"ctx": lax.rem(me + 1, window)},
    )
    send_far = pltpu.make_async_remote_copy(
        src_ref=kv.at[last], dst_ref=far, send_sem=far_sem.at[0], recv_sem=far_sem.at[1],
        device_id={"ctx": lax.rem(me + 2, window)},
    )

    @pl.when(me + 1 < window)
    def _():
        send_near.start()

    @pl.when(me + 2 < window)
    def _():
        send_far.start()

    def await_request(source, carry):
        asked(source).wait_recv()
        return carry

    lax.fori_loop(me + 1, window, await_request, 0)
    to_scalars = pltpu.make_async_copy(requests, scalars, scalar_sem)
    to_scalars.start()
    to_scalars.wait()

    def answer(other, at, slot):
        return pltpu.make_async_remote_copy(
            src_ref=answers.at[at], dst_ref=landed.at[slot], send_sem=answer_send.at[at], recv_sem=answer_recv.at[slot],
            device_id={"ctx": other},
        )

    def start_answer(j, carry):
        other = flip(me, window - 1 - j, window)

        @pl.when(other > me)
        def _():
            for c in range(cap):
                answers[other, c] = kv[scalars[other, 0, me * cap + c]]
            answer(other, other, me).start()

        return carry

    lax.fori_loop(0, window - 1, start_answer, 0)

    @pl.when(me >= 1)
    def _():
        send_near.wait_recv()

    @pl.when(me >= 2)
    def _():
        send_far.wait_recv()

    width = LOCAL_BAND_SIZE * BLOCK_TOKENS
    factor = HEAD_SIZE**-0.5 * log2_e
    row = lax.broadcasted_iota(jnp.int32, (BLOCK_TOKENS, width), 0)
    column = lax.broadcasted_iota(jnp.int32, (BLOCK_TOKENS, width), 1)
    lane = lax.broadcasted_iota(jnp.int32, (BLOCK_TOKENS, 128), 1)

    def store(h):
        return [
            pltpu.make_async_copy(rotated_held.at[h], rotated.at[h], store_sem.at[0, h]),
            pltpu.make_async_copy(partial_held.at[h], partial.at[h], store_sem.at[1, h]),
            pltpu.make_async_copy(stats_held.at[h], stats.at[h], store_sem.at[2, h]),
        ]

    def one_head(h, carry):
        load(h).wait()
        band = [far[h]] + [near[i * KEY_VALUE_HEADS + h] for i in range(blocks)]
        band = band + [kv[i * KEY_VALUE_HEADS + h] for i in range(blocks)]
        k_all = jnp.concatenate([b[0] for b in band], 0)
        v_all = with_ones(jnp.concatenate([b[1] for b in band], 0))
        for i in range(blocks):
            start = (me * blocks + i - (LOCAL_BAND_SIZE - 1)) * BLOCK_TOKENS
            good = (column <= row + (LOCAL_BAND_SIZE - 1) * BLOCK_TOKENS) & (column + start >= 0)
            bias = jnp.where(good, 0.0, masked_score)
            rows = slice(i * BLOCK_TOKENS, (i + 1) * BLOCK_TOKENS)
            k = k_all[i * BLOCK_TOKENS : i * BLOCK_TOKENS + width]
            v = v_all[i * BLOCK_TOKENS : i * BLOCK_TOKENS + width]
            q_cosine, q_sine = cosine[rows] * factor, sine[rows] * factor
            held = jnp.zeros((BLOCK_TOKENS, 128), jnp.float32)
            for n in range(GROUP):
                columns = slice(n * HEAD_SIZE, (n + 1) * HEAD_SIZE)
                q = rotate(q_held[h, rows, columns], q_cosine, q_sine).astype(jnp.bfloat16)
                rotated_held[h, rows, columns] = q
                score = dot_nt(q, k) + bias
                top = jnp.max(score, 1, keepdims=True)
                weight = jnp.exp2(score - top).astype(jnp.bfloat16)
                summed = jnp.dot(weight, v, preferred_element_type=jnp.float32)
                total = summed[:, HEAD_SIZE:]
                partial_held[h, rows, columns] = (summed[:, :HEAD_SIZE] / total).astype(jnp.bfloat16)
                held = jnp.where(lane == n, top + jnp.log2(total), held)
            stats_held[h, rows] = held
        for copy in store(h):
            copy.start()
        return carry

    lax.fori_loop(0, KEY_VALUE_HEADS, one_head, 0)

    def end_store(h, carry):
        for copy in store(h):
            copy.wait()
        return carry

    lax.fori_loop(0, KEY_VALUE_HEADS, end_store, 0)

    @pl.when(me + 1 < window)
    def _():
        send_near.wait_send()

    @pl.when(me + 2 < window)
    def _():
        send_far.wait_send()

    def end_ask(owner, carry):
        ask(owner).wait_send()
        return carry

    lax.fori_loop(0, me, end_ask, 0)

    def end_answer(other, carry):
        answer(other, other, me).wait_send()
        return carry

    lax.fori_loop(me + 1, window, end_answer, 0)

    def arrive(source, carry):
        answer(source, source, source).wait_recv()
        return carry

    lax.fori_loop(0, me, arrive, 0)


def pick_kernel(blocks, slots, rotated, partial, stats, *rest):
    landed, out = rest[:-1], rest[-1]
    head = pl.program_id(0)
    column = lax.broadcasted_iota(jnp.int32, (1, PICKED_BLOCKS * BLOCK_TOKENS), 1)
    for i in range(blocks):
        ks, vs = [], []
        bias = jnp.zeros(column.shape, jnp.float32)
        for p in range(PICKED_BLOCKS):
            at = (i * KEY_VALUE_HEADS + head) * PICKED_BLOCKS + p
            alive = slots[0, at] >= 0
            pair = landed[i * PICKED_BLOCKS + p]
            ks.append(jnp.where(alive, pair[0, 0], jnp.zeros_like(pair[0, 0])))
            vs.append(jnp.where(alive, pair[0, 1], jnp.zeros_like(pair[0, 1])))
            bias = jnp.where(column // BLOCK_TOKENS == p, jnp.where(alive, 0.0, masked_score), bias)
        k = jnp.concatenate(ks, 0)
        v = with_ones(jnp.concatenate(vs, 0))
        rows = slice(i * BLOCK_TOKENS, (i + 1) * BLOCK_TOKENS)
        score = dot_nt(stack_heads(rotated[0, rows]), k) + bias
        near_top = jnp.concatenate([stats[0, rows, n : n + 1] for n in range(GROUP)], 0)
        top = jnp.maximum(jnp.max(score, 1, keepdims=True), near_top)
        weight = jnp.exp2(score - top).astype(jnp.bfloat16)
        summed = jnp.dot(weight, v, preferred_element_type=jnp.float32)
        near_weight = jnp.exp2(near_top - top)
        held = stack_heads(partial[0, rows]).astype(jnp.float32)
        result = (held * near_weight + summed[:, :HEAD_SIZE]) / (near_weight + summed[:, HEAD_SIZE:])
        result = result.astype(jnp.bfloat16)
        for n in range(GROUP):
            out[rows, n * HEAD_SIZE : (n + 1) * HEAD_SIZE] = result[head_rows(n)]


def shards(queries, keys, values, positions, picks):
    tokens = queries.shape[0]
    blocks = tokens // BLOCK_TOKENS
    window = lax.axis_size("ctx")
    cap = max(1, blocks * KEY_VALUE_HEADS * PICKED_BLOCKS // window)
    per_head = GROUP * HEAD_SIZE
    entries = blocks * KEY_VALUE_HEADS
    count = entries * PICKED_BLOCKS
    lanes = -(-window * cap // 128) * 128

    half = HEAD_SIZE // 2
    freq = rope_base ** (-(jnp.arange(half, dtype=jnp.float32) * 2.0) / HEAD_SIZE)
    angle = positions.astype(jnp.float32)[:, None] * freq[None, :]
    cosine, sine = jnp.cos(angle), jnp.sin(angle)
    cosine = jnp.concatenate([cosine, cosine], 1)
    sine = jnp.concatenate([-sine, sine], 1)

    here = pl.BlockSpec(memory_space=pltpu.VMEM)
    there = pl.BlockSpec(memory_space=pl.ANY)
    by_head = (KEY_VALUE_HEADS, tokens, per_head)
    stats_dims = (KEY_VALUE_HEADS, tokens, 128)
    width = LOCAL_BAND_SIZE * BLOCK_TOKENS
    limit = 56 * 1024 * 1024
    rotated, partial, stats, landed, slots = pl.pallas_call(
        functools.partial(exchange_kernel, blocks, window, cap),
        in_specs=[there] + [here] * 6,
        out_specs=[there] * 4 + [here],
        out_shape=[
            jax.ShapeDtypeStruct(by_head, jnp.bfloat16),
            jax.ShapeDtypeStruct(by_head, jnp.bfloat16),
            jax.ShapeDtypeStruct(stats_dims, jnp.float32),
            jax.ShapeDtypeStruct((window, cap) + ENTRY, jnp.bfloat16),
            jax.ShapeDtypeStruct((1, count), jnp.int32),
        ],
        scratch_shapes=[
            pltpu.VMEM(by_head, jnp.bfloat16),
            pltpu.VMEM(by_head, jnp.bfloat16),
            pltpu.VMEM(by_head, jnp.bfloat16),
            pltpu.VMEM(stats_dims, jnp.float32),
            pltpu.VMEM((entries,) + ENTRY, jnp.bfloat16),
            pltpu.VMEM((entries,) + ENTRY, jnp.bfloat16),
            pltpu.VMEM((KEY_VALUE_HEADS,) + ENTRY, jnp.bfloat16),
            pltpu.VMEM((window, cap) + ENTRY, jnp.bfloat16),
            pltpu.VMEM((1, lanes), jnp.int32),
            pltpu.VMEM((window, 1, lanes), jnp.int32),
            pltpu.SMEM((window, 1, lanes), jnp.int32),
            pltpu.SemaphoreType.DMA((KEY_VALUE_HEADS,)),
            pltpu.SemaphoreType.DMA((3, KEY_VALUE_HEADS)),
            pltpu.SemaphoreType.DMA((2,)),
            pltpu.SemaphoreType.DMA((2,)),
            pltpu.SemaphoreType.DMA((window,)),
            pltpu.SemaphoreType.DMA((window,)),
            pltpu.SemaphoreType.DMA,
            pltpu.SemaphoreType.DMA((window,)),
            pltpu.SemaphoreType.DMA((window,)),
        ],
        compiler_params=pltpu.CompilerParams(collective_id=0, has_side_effects=True, vmem_limit_bytes=limit),
        cost_estimate=pl.CostEstimate(
            flops=4 * tokens * QUERY_HEADS * HEAD_SIZE * width,
            bytes_accessed=tokens * QUERY_HEADS * HEAD_SIZE * 6,
            transcendentals=tokens * QUERY_HEADS * width,
        ),
        name="exchange_and_band",
    )(queries, keys, values, cosine, sine, picks.reshape(1, count), picks.reshape(count, 1))

    def slot_spec(i, p):
        def place(h, slot):
            return (jnp.maximum(slot[0, (i * KEY_VALUE_HEADS + h) * PICKED_BLOCKS + p], 0), 0, 0, 0)

        return pl.BlockSpec((1,) + ENTRY, place)

    by_head_spec = pl.BlockSpec((1, tokens, per_head), lambda h, *_: (h, 0, 0))
    landed = landed.reshape((window * cap,) + ENTRY)
    return pl.pallas_call(
        functools.partial(pick_kernel, blocks),
        grid_spec=pltpu.PrefetchScalarGridSpec(
            num_scalar_prefetch=1,
            grid=(KEY_VALUE_HEADS,),
            in_specs=[by_head_spec, by_head_spec, pl.BlockSpec((1, tokens, 128), lambda h, *_: (h, 0, 0))]
            + [slot_spec(i, p) for i in range(blocks) for p in range(PICKED_BLOCKS)],
            out_specs=pl.BlockSpec((tokens, per_head), lambda h, *_: (0, h)),
        ),
        out_shape=jax.ShapeDtypeStruct(queries.shape, jnp.bfloat16),
        compiler_params=pltpu.CompilerParams(vmem_limit_bytes=limit),
        name="picked_attention",
    )(slots, rotated, partial, stats, *[landed] * (blocks * PICKED_BLOCKS))


def solution(mesh):
    rows = P(("groups", "ctx"), None)
    return jax.shard_map(
        shards,
        mesh=mesh,
        in_specs=(rows, rows, rows, P(("groups", "ctx")), P(("groups", "ctx"), None, None)),
        out_specs=rows,
        check_vma=False,
    )
```

```python
import functools

import jax
import jax.numpy as jnp
from jax import lax
from jax.experimental import pallas as pl
from jax.experimental.pallas import tpu as pltpu
from jax.sharding import PartitionSpec as P

QUERY_HEADS = 64
KEY_VALUE_HEADS = 8
HEAD_SIZE = 128
BLOCK_TOKENS = 128
LOCAL_BAND_SIZE = 4
PICKED_BLOCKS = 2
GROUP = QUERY_HEADS // KEY_VALUE_HEADS
ENTRY = (2, BLOCK_TOKENS, HEAD_SIZE)

rope_base = 500000.0
masked_score = -1e30
log2_e = 1.4426950408889634


def rotate(x, cosine, sine):
    wide = x.astype(jnp.float32)
    return wide * cosine + pltpu.roll(wide, HEAD_SIZE // 2, 1) * sine


def dot_nt(a, b):
    return lax.dot_general(a, b, (((1,), (1,)), ((), ())), preferred_element_type=jnp.float32)


def with_ones(v):
    return jnp.concatenate([v, jnp.ones((16, v.shape[1]), v.dtype)], 0)


CHUNK = 4


def flip(a, b, size):
    out, bit = 0, 1
    while bit < size:
        out = out + (a // bit + b // bit) % 2 * bit
        bit *= 2
    return out


def exchange_kernel(
    blocks, window, cap, relays,
    queries, keys, values, cosine, sine, pick_row,
    rotated, partial, stats, landed, slots,
    q_held, rotated_held, partial_held, stats_held, kv, near, far, relay_a, relay_b, answers, request, requests, scalars,
    load_sem, store_sem, near_send, near_recv, far_send, far_recv, relay_send, relay_recv, forward_send, chip_send, request_send, request_recv, scalar_sem, answer_send, answer_recv,
):
    me = lax.axis_index("ctx")
    count = pick_row.shape[1]
    per_head = GROUP * HEAD_SIZE
    barrier = pltpu.get_barrier_semaphore()

    def greet(j, carry):
        pl.semaphore_signal(barrier, inc=1, device_id={"ctx": lax.rem(me + j, window)})
        return carry

    lax.fori_loop(1, window, greet, 0)

    def load(h):
        columns = pl.ds(pl.multiple_of(h * per_head, per_head), per_head)
        return pltpu.make_async_copy(queries.at[:, columns], q_held.at[h], load_sem.at[h])

    def start_load(h, carry):
        load(h).start()
        return carry

    lax.fori_loop(0, KEY_VALUE_HEADS, start_load, 0)

    row = pick_row[...]
    first = lax.broadcasted_iota(jnp.int32, (count, count), 0)
    second = lax.broadcasted_iota(jnp.int32, (count, count), 1)
    column = jnp.sum(jnp.where(first == second, row, 0), 1, keepdims=True)
    row_owner = jnp.maximum(row, 0) // blocks
    column_owner = jnp.maximum(column, 0) // blocks
    alike = (column_owner == row_owner) & (column >= 0) & (row >= 0)
    column_rank = jnp.sum((alike & (second < first)).astype(jnp.int32), 1, keepdims=True)
    row_rank = jnp.sum((alike & (first < second)).astype(jnp.int32), 0, keepdims=True)
    slots[...] = jnp.where(row >= 0, row_owner * cap + jnp.minimum(row_rank, cap - 1), -1)
    order = lax.broadcasted_iota(jnp.int32, (count, 1), 0)
    entry = jnp.maximum(column, 0) % blocks * KEY_VALUE_HEADS + order // PICKED_BLOCKS % KEY_VALUE_HEADS
    lane = lax.broadcasted_iota(jnp.int32, (count, request.shape[1]), 1)
    hit = (column_owner * cap + column_rank == lane) & (column >= 0)
    request[...] = jnp.sum(jnp.where(hit, entry, 0), 0, keepdims=True)

    for i in range(blocks):
        rows = slice(i * BLOCK_TOKENS, (i + 1) * BLOCK_TOKENS)
        for head in range(KEY_VALUE_HEADS):
            columns = slice(head * HEAD_SIZE, (head + 1) * HEAD_SIZE)
            kv[i * KEY_VALUE_HEADS + head, 0] = rotate(keys[rows, columns], cosine[rows], sine[rows]).astype(jnp.bfloat16)
            kv[i * KEY_VALUE_HEADS + head, 1] = values[rows, columns].astype(jnp.float32).T.astype(jnp.bfloat16)

    @pl.when(me < 1)
    def _():
        near[...] = jnp.zeros_like(near)

    @pl.when(me < 2)
    def _():
        far[...] = jnp.zeros_like(far)

    pl.semaphore_wait(barrier, window - 1)

    def ask(owner):
        return pltpu.make_async_remote_copy(
            src_ref=request, dst_ref=requests.at[me], send_sem=request_send.at[owner], recv_sem=request_recv.at[me],
            device_id={"ctx": owner},
        )

    def asked(source):
        return pltpu.make_async_remote_copy(
            src_ref=request, dst_ref=requests.at[source], send_sem=request_send.at[source],
            recv_sem=request_recv.at[source], device_id={"ctx": source},
        )

    def start_ask(owner, carry):
        ask(owner).start()
        return carry

    lax.fori_loop(0, me, start_ask, 0)

    def put(source, target, send_sem, recv_sem, to):
        return pltpu.make_async_remote_copy(
            src_ref=source, dst_ref=target, send_sem=send_sem, recv_sem=recv_sem,
            device_id={"ctx": lax.rem(to + window, window)},
        )

    last = (blocks - 1) * KEY_VALUE_HEADS
    near_part, far_part = blocks * KEY_VALUE_HEADS // 2, KEY_VALUE_HEADS // 2

    def near_at(ref, half):
        return ref.at[pl.ds(half * near_part, near_part)]

    def far_at(ref, half, base=0):
        return ref.at[pl.ds(base + half * far_part, far_part)]

    def both(copies):
        return [copies(half) for half in range(2)]

    near_direct = both(lambda h: put(near_at(kv, h), near_at(near, h), near_send.at[h], near_recv.at[h], me + 1))
    far_direct = both(lambda h: put(far_at(kv, h, last), far_at(far, h), far_send.at[h], far_recv.at[h], me + 2))
    if relays:
        core, x, z = me % 2, me // 2 % 2, me // 4
        rows_z = window // 4
        to_relay = [(me - 2, relay_a), (me + 4, relay_b)]
        near_out = both(lambda h: put(near_at(kv, h), to_relay[h][1], relay_send.at[h], relay_recv.at[h], to_relay[h][0]))
        far_out = both(
            lambda h: put(
                far_at(kv, h, last), far_at(to_relay[h][1], 0), relay_send.at[h], relay_recv.at[h], to_relay[h][0]
            )
        )
        near_targets, far_targets = (me + 3, me - 3), (me + 4, me - 2)
        relay_refs = (relay_a, relay_b)
        near_on = both(
            lambda h: put(relay_refs[h], near_at(near, h), forward_send.at[h], near_recv.at[h], near_targets[h])
        )
        far_on = both(
            lambda h: put(far_at(relay_refs[h], 0), far_at(far, h), forward_send.at[h], far_recv.at[h], far_targets[h])
        )
        chip_far = both(lambda h: put(far_at(near, h, last), far_at(far, h), chip_send.at[h], far_recv.at[h], me + 1))
        now = [
            ((x == 1) & (core == 1) & (z < rows_z - 1), near_out),
            ((x == 1) & (core == 0) & (z < rows_z - 1), far_out),
            ((core == 1) & (x == 0), near_direct),
            ((core == 0) & (x == 0), far_direct),
            (core == 0, near_direct),
        ]
        as_relay = [((x == 0) & (z < rows_z - 1)), ((x == 1) & (z > 0))]
        as_forwarder = (core == 0) & (me >= 2)
    else:
        now = [(me + 1 < window, near_direct), (me + 2 < window, far_direct)]

    for condition, copies in now:

        @pl.when(condition)
        def _(copies=copies):
            for copy in copies:
                copy.start()

    def await_request(source, carry):
        asked(source).wait_recv()
        return carry

    lax.fori_loop(me + 1, window, await_request, 0)
    to_scalars = pltpu.make_async_copy(requests, scalars, scalar_sem)
    to_scalars.start()
    to_scalars.wait()

    def answer(other, at, slot):
        return pltpu.make_async_remote_copy(
            src_ref=answers.at[at], dst_ref=landed.at[slot], send_sem=answer_send.at[at], recv_sem=answer_recv.at[slot],
            device_id={"ctx": other},
        )

    def start_answer(j, carry):
        other = flip(me, window - 1 - j, window)

        @pl.when(other > me)
        def _():
            for c in range(cap):
                answers[other, c] = kv[scalars[other, 0, me * cap + c]]
            answer(other, other, me).start()

        return carry

    lax.fori_loop(0, window - 1, start_answer, 0)

    if relays:
        for half in range(2):
            for at_core, arriving, on in ((1, near_out, near_on), (0, far_out, far_on)):

                @pl.when(as_relay[half] & (core == at_core))
                def _(half=half, arriving=arriving, on=on):
                    arriving[half].wait_recv()
                    on[half].start()

    @pl.when(me >= 1)
    def _():
        for copy in near_direct:
            copy.wait_recv()

    if relays:

        @pl.when(as_forwarder)
        def _():
            for copy in chip_far:
                copy.start()

    @pl.when(me >= 2)
    def _():
        for copy in far_direct:
            copy.wait_recv()

    width = LOCAL_BAND_SIZE * BLOCK_TOKENS
    factor = HEAD_SIZE**-0.5 * log2_e
    key = lax.broadcasted_iota(jnp.int32, (width, BLOCK_TOKENS), 0)
    query = lax.broadcasted_iota(jnp.int32, (width, BLOCK_TOKENS), 1)

    def store(h):
        return [
            pltpu.make_async_copy(rotated_held.at[h], rotated.at[h], store_sem.at[0, h]),
            pltpu.make_async_copy(partial_held.at[h], partial.at[h], store_sem.at[1, h]),
            pltpu.make_async_copy(stats_held.at[h], stats.at[h], store_sem.at[2, h]),
        ]

    def one_head(h, carry):
        load(h).wait()
        band = [far[h]] + [near[i * KEY_VALUE_HEADS + h] for i in range(blocks)]
        band = band + [kv[i * KEY_VALUE_HEADS + h] for i in range(blocks)]
        k_all = jnp.concatenate([b[0] for b in band], 0)
        v_all = with_ones(jnp.concatenate([b[1] for b in band], 1))
        for i in range(blocks):
            start = (me * blocks + i - (LOCAL_BAND_SIZE - 1)) * BLOCK_TOKENS
            good = (key <= query + (LOCAL_BAND_SIZE - 1) * BLOCK_TOKENS) & (key + start >= 0)
            bias = jnp.concatenate([jnp.where(good, 0.0, masked_score)] * CHUNK, 1)
            rows = slice(i * BLOCK_TOKENS, (i + 1) * BLOCK_TOKENS)
            k = k_all[i * BLOCK_TOKENS : i * BLOCK_TOKENS + width]
            v = v_all[:, i * BLOCK_TOKENS : i * BLOCK_TOKENS + width]
            q_cosine, q_sine = cosine[rows] * factor, sine[rows] * factor
            for part in range(GROUP // CHUNK):
                here = slice(part * CHUNK * BLOCK_TOKENS, (part + 1) * CHUNK * BLOCK_TOKENS)
                heads = range(part * CHUNK, (part + 1) * CHUNK)
                q = jnp.concatenate(
                    [rotate(q_held[h, rows, n * HEAD_SIZE : (n + 1) * HEAD_SIZE], q_cosine, q_sine) for n in heads], 0
                ).astype(jnp.bfloat16)
                rotated_held[h, i, here] = q
                score = dot_nt(k, q) + bias
                top = jnp.max(score, 0, keepdims=True)
                weight = jnp.exp2(score - top).astype(jnp.bfloat16)
                summed = jnp.dot(v, weight, preferred_element_type=jnp.float32)
                total = summed[HEAD_SIZE : HEAD_SIZE + 1]
                partial_held[h, i, :, here] = (summed[:HEAD_SIZE] * (1.0 / total)).astype(jnp.bfloat16)
                stats_held[h, i, :, here] = top + jnp.log2(total)
        for copy in store(h):
            copy.start()
        return carry

    lax.fori_loop(0, KEY_VALUE_HEADS, one_head, 0)

    def end_store(h, carry):
        for copy in store(h):
            copy.wait()
        return carry

    lax.fori_loop(0, KEY_VALUE_HEADS, end_store, 0)

    for condition, copies in now:

        @pl.when(condition)
        def _(copies=copies):
            for copy in copies:
                copy.wait_send()

    if relays:
        for half in range(2):
            for at_core, on in ((1, near_on), (0, far_on)):

                @pl.when(as_relay[half] & (core == at_core))
                def _(half=half, on=on):
                    on[half].wait_send()

        @pl.when(as_forwarder)
        def _():
            for copy in chip_far:
                copy.wait_send()

    def end_ask(owner, carry):
        ask(owner).wait_send()
        return carry

    lax.fori_loop(0, me, end_ask, 0)

    def end_answer(other, carry):
        answer(other, other, me).wait_send()
        return carry

    lax.fori_loop(me + 1, window, end_answer, 0)

    def arrive(source, carry):
        answer(source, source, source).wait_recv()
        return carry

    lax.fori_loop(0, me, arrive, 0)


def pick_kernel(blocks, slots, rotated, partial, stats, *rest):
    landed, out = rest[:-1], rest[-1]
    head = pl.program_id(0)
    for i in range(blocks):
        alive = slots[0, (i * KEY_VALUE_HEADS + head) * PICKED_BLOCKS] >= 0
        rows = slice(i * BLOCK_TOKENS, (i + 1) * BLOCK_TOKENS)

        def give(part, result):
            for n in range(CHUNK):
                at = (part * CHUNK + n) * HEAD_SIZE
                out[rows, at : at + HEAD_SIZE] = result[:, n * BLOCK_TOKENS : (n + 1) * BLOCK_TOKENS].T.astype(jnp.bfloat16)

        @pl.when(alive)
        def _():
            pair = landed[i * PICKED_BLOCKS : (i + 1) * PICKED_BLOCKS]
            k = jnp.concatenate([p[0, 0] for p in pair], 0)
            v = with_ones(jnp.concatenate([p[0, 1] for p in pair], 1))
            for part in range(GROUP // CHUNK):
                here = slice(part * CHUNK * BLOCK_TOKENS, (part + 1) * CHUNK * BLOCK_TOKENS)
                score = dot_nt(k, rotated[0, i, here])
                near_top = stats[0, i, :, here]
                top = jnp.maximum(jnp.max(score, 0, keepdims=True), near_top)
                weight = jnp.exp2(score - top).astype(jnp.bfloat16)
                summed = jnp.dot(v, weight, preferred_element_type=jnp.float32)
                near_weight = jnp.exp2(near_top - top)
                inverse = 1.0 / (near_weight + summed[HEAD_SIZE : HEAD_SIZE + 1])
                held = partial[0, i, :, here].astype(jnp.float32)
                give(part, held * (near_weight * inverse) + summed[:HEAD_SIZE] * inverse)

        @pl.when(jnp.logical_not(alive))
        def _():
            for part in range(GROUP // CHUNK):
                here = slice(part * CHUNK * BLOCK_TOKENS, (part + 1) * CHUNK * BLOCK_TOKENS)
                give(part, partial[0, i, :, here].astype(jnp.float32))


def shards(queries, keys, values, positions, picks):
    tokens = queries.shape[0]
    blocks = tokens // BLOCK_TOKENS
    window = lax.axis_size("ctx")
    cap = max(1, blocks * KEY_VALUE_HEADS * PICKED_BLOCKS // window)
    per_head = GROUP * HEAD_SIZE
    entries = blocks * KEY_VALUE_HEADS
    count = entries * PICKED_BLOCKS
    lanes = -(-window * cap // 128) * 128

    half = HEAD_SIZE // 2
    freq = rope_base ** (-(jnp.arange(half, dtype=jnp.float32) * 2.0) / HEAD_SIZE)
    angle = positions.astype(jnp.float32)[:, None] * freq[None, :]
    cosine, sine = jnp.cos(angle), jnp.sin(angle)
    cosine = jnp.concatenate([cosine, cosine], 1)
    sine = jnp.concatenate([-sine, sine], 1)

    here = pl.BlockSpec(memory_space=pltpu.VMEM)
    there = pl.BlockSpec(memory_space=pl.ANY)
    by_head = (KEY_VALUE_HEADS, tokens, per_head)
    stacked = GROUP * BLOCK_TOKENS
    rotated_dims = (KEY_VALUE_HEADS, blocks, stacked, HEAD_SIZE)
    partial_dims = (KEY_VALUE_HEADS, blocks, HEAD_SIZE, stacked)
    stats_dims = (KEY_VALUE_HEADS, blocks, 1, stacked)
    width = LOCAL_BAND_SIZE * BLOCK_TOKENS
    limit = 56 * 1024 * 1024
    rotated, partial, stats, landed, slots = pl.pallas_call(
        functools.partial(exchange_kernel, blocks, window, cap, window == 16),
        in_specs=[there] + [here] * 5,
        out_specs=[there] * 4 + [here],
        out_shape=[
            jax.ShapeDtypeStruct(rotated_dims, jnp.bfloat16),
            jax.ShapeDtypeStruct(partial_dims, jnp.bfloat16),
            jax.ShapeDtypeStruct(stats_dims, jnp.float32),
            jax.ShapeDtypeStruct((window, cap) + ENTRY, jnp.bfloat16),
            jax.ShapeDtypeStruct((1, count), jnp.int32),
        ],
        scratch_shapes=[
            pltpu.VMEM(by_head, jnp.bfloat16),
            pltpu.VMEM(rotated_dims, jnp.bfloat16),
            pltpu.VMEM(partial_dims, jnp.bfloat16),
            pltpu.VMEM(stats_dims, jnp.float32),
            pltpu.VMEM((entries,) + ENTRY, jnp.bfloat16),
            pltpu.VMEM((entries,) + ENTRY, jnp.bfloat16),
            pltpu.VMEM((KEY_VALUE_HEADS,) + ENTRY, jnp.bfloat16),
            pltpu.VMEM((entries // 2,) + ENTRY, jnp.bfloat16),
            pltpu.VMEM((entries // 2,) + ENTRY, jnp.bfloat16),
            pltpu.VMEM((window, cap) + ENTRY, jnp.bfloat16),
            pltpu.VMEM((1, lanes), jnp.int32),
            pltpu.VMEM((window, 1, lanes), jnp.int32),
            pltpu.SMEM((window, 1, lanes), jnp.int32),
            pltpu.SemaphoreType.DMA((KEY_VALUE_HEADS,)),
            pltpu.SemaphoreType.DMA((3, KEY_VALUE_HEADS)),
            pltpu.SemaphoreType.DMA((2,)),
            pltpu.SemaphoreType.DMA((2,)),
            pltpu.SemaphoreType.DMA((2,)),
            pltpu.SemaphoreType.DMA((2,)),
            pltpu.SemaphoreType.DMA((2,)),
            pltpu.SemaphoreType.DMA((2,)),
            pltpu.SemaphoreType.DMA((2,)),
            pltpu.SemaphoreType.DMA((2,)),
            pltpu.SemaphoreType.DMA((window,)),
            pltpu.SemaphoreType.DMA((window,)),
            pltpu.SemaphoreType.DMA,
            pltpu.SemaphoreType.DMA((window,)),
            pltpu.SemaphoreType.DMA((window,)),
        ],
        compiler_params=pltpu.CompilerParams(collective_id=0, has_side_effects=True, vmem_limit_bytes=limit),
        cost_estimate=pl.CostEstimate(
            flops=4 * tokens * QUERY_HEADS * HEAD_SIZE * width,
            bytes_accessed=tokens * QUERY_HEADS * HEAD_SIZE * 6,
            transcendentals=tokens * QUERY_HEADS * width,
        ),
        name="exchange_and_band",
    )(queries, keys, values, cosine, sine, picks.reshape(1, count))

    def slot_spec(i, p):
        def place(h, slot):
            return (jnp.maximum(slot[0, (i * KEY_VALUE_HEADS + h) * PICKED_BLOCKS + p], 0), 0, 0, 0)

        return pl.BlockSpec((1,) + ENTRY, place)

    def head_spec(dims):
        return pl.BlockSpec((1,) + dims[1:], lambda h, *_: (h, 0, 0, 0))

    landed = landed.reshape((window * cap,) + ENTRY)
    return pl.pallas_call(
        functools.partial(pick_kernel, blocks),
        grid_spec=pltpu.PrefetchScalarGridSpec(
            num_scalar_prefetch=1,
            grid=(KEY_VALUE_HEADS,),
            in_specs=[head_spec(rotated_dims), head_spec(partial_dims), head_spec(stats_dims)]
            + [slot_spec(i, p) for i in range(blocks) for p in range(PICKED_BLOCKS)],
            out_specs=pl.BlockSpec((tokens, per_head), lambda h, *_: (0, h)),
        ),
        out_shape=jax.ShapeDtypeStruct(queries.shape, jnp.bfloat16),
        compiler_params=pltpu.CompilerParams(vmem_limit_bytes=limit),
        name="picked_attention",
    )(slots, rotated, partial, stats, *[landed] * (blocks * PICKED_BLOCKS))


def solution(mesh):
    rows = P(("groups", "ctx"), None)
    return jax.shard_map(
        shards,
        mesh=mesh,
        in_specs=(rows, rows, rows, P(("groups", "ctx")), P(("groups", "ctx"), None, None)),
        out_specs=rows,
        check_vma=False,
    )
```

```python
import functools

import jax
import jax.numpy as jnp
from jax import lax
from jax.experimental import pallas as pl
from jax.experimental.pallas import tpu as pltpu
from jax.sharding import PartitionSpec as P

QUERY_HEADS = 64
KEY_VALUE_HEADS = 8
HEAD_SIZE = 128
BLOCK_TOKENS = 128
LOCAL_BAND_SIZE = 4
PICKED_BLOCKS = 2
GROUP = QUERY_HEADS // KEY_VALUE_HEADS
ENTRY = (2, BLOCK_TOKENS, HEAD_SIZE)

rope_base = 500000.0
masked_score = -1e30
log2_e = 1.4426950408889634


def rotate(x, cosine, sine):
    wide = x.astype(jnp.float32)
    return wide * cosine + pltpu.roll(wide, HEAD_SIZE // 2, 1) * sine


def dot_nt(a, b):
    return lax.dot_general(a, b, (((1,), (1,)), ((), ())), preferred_element_type=jnp.float32)


def with_ones(v):
    return jnp.concatenate([v, jnp.ones((16, v.shape[1]), v.dtype)], 0)


CHUNK = 4


def flip(a, b, size):
    out, bit = 0, 1
    while bit < size:
        out = out + (a // bit + b // bit) % 2 * bit
        bit *= 2
    return out


def exchange_kernel(
    blocks, window, cap, relays,
    queries, keys, values, cosine, sine, pick_row,
    partial, stats, slot_partial, slot_stats, slots,
    q_held, rotated, partial_held, stats_held, slot_partial_held, slot_stats_held, landed, kv, near, far, relay_a, relay_b, answers, request, requests, scalars, users, user_scalars,
    load_sem, store_sem, near_send, near_recv, far_send, far_recv, relay_send, relay_recv, forward_send, chip_send, request_send, request_recv, scalar_sem, slot_sem, answer_send, answer_recv,
):
    me = lax.axis_index("ctx")
    count = pick_row.shape[1]
    per_head = GROUP * HEAD_SIZE
    barrier = pltpu.get_barrier_semaphore()

    def greet(j, carry):
        pl.semaphore_signal(barrier, inc=1, device_id={"ctx": lax.rem(me + j, window)})
        return carry

    lax.fori_loop(1, window, greet, 0)

    def load(h):
        columns = pl.ds(pl.multiple_of(h * per_head, per_head), per_head)
        return pltpu.make_async_copy(queries.at[:, columns], q_held.at[h], load_sem.at[h])

    def start_load(h, carry):
        load(h).start()
        return carry

    lax.fori_loop(0, KEY_VALUE_HEADS, start_load, 0)

    row = pick_row[...]
    first = lax.broadcasted_iota(jnp.int32, (count, count), 0)
    second = lax.broadcasted_iota(jnp.int32, (count, count), 1)
    column = jnp.sum(jnp.where(first == second, row, 0), 1, keepdims=True)
    row_owner = jnp.maximum(row, 0) // blocks
    column_owner = jnp.maximum(column, 0) // blocks
    alike = (column_owner == row_owner) & (column >= 0) & (row >= 0)
    column_rank = jnp.sum((alike & (second < first)).astype(jnp.int32), 1, keepdims=True)
    row_rank = jnp.sum((alike & (first < second)).astype(jnp.int32), 0, keepdims=True)
    slots[...] = jnp.where(row >= 0, row_owner * cap + jnp.minimum(row_rank, cap - 1), -1)
    order = lax.broadcasted_iota(jnp.int32, (count, 1), 0)
    entry = jnp.maximum(column, 0) % blocks * KEY_VALUE_HEADS + order // PICKED_BLOCKS % KEY_VALUE_HEADS
    lane = lax.broadcasted_iota(jnp.int32, (count, request.shape[1]), 1)
    hit = (column_owner * cap + column_rank == lane) & (column >= 0)
    request[...] = jnp.sum(jnp.where(hit, entry, 0), 0, keepdims=True)
    users[...] = jnp.sum(jnp.where(hit, order // PICKED_BLOCKS, 0), 0, keepdims=True)

    for i in range(blocks):
        rows = slice(i * BLOCK_TOKENS, (i + 1) * BLOCK_TOKENS)
        for head in range(KEY_VALUE_HEADS):
            columns = slice(head * HEAD_SIZE, (head + 1) * HEAD_SIZE)
            kv[i * KEY_VALUE_HEADS + head, 0] = rotate(keys[rows, columns], cosine[rows], sine[rows]).astype(jnp.bfloat16)
            kv[i * KEY_VALUE_HEADS + head, 1] = values[rows, columns].astype(jnp.float32).T.astype(jnp.bfloat16)

    @pl.when(me < 1)
    def _():
        near[...] = jnp.zeros_like(near)

    @pl.when(me < 2)
    def _():
        far[...] = jnp.zeros_like(far)

    pl.semaphore_wait(barrier, window - 1)

    def ask(owner):
        return pltpu.make_async_remote_copy(
            src_ref=request, dst_ref=requests.at[me], send_sem=request_send.at[owner], recv_sem=request_recv.at[me],
            device_id={"ctx": owner},
        )

    def asked(source):
        return pltpu.make_async_remote_copy(
            src_ref=request, dst_ref=requests.at[source], send_sem=request_send.at[source],
            recv_sem=request_recv.at[source], device_id={"ctx": source},
        )

    def start_ask(owner, carry):
        ask(owner).start()
        return carry

    lax.fori_loop(0, me, start_ask, 0)

    def put(source, target, send_sem, recv_sem, to):
        return pltpu.make_async_remote_copy(
            src_ref=source, dst_ref=target, send_sem=send_sem, recv_sem=recv_sem,
            device_id={"ctx": lax.rem(to + window, window)},
        )

    last = (blocks - 1) * KEY_VALUE_HEADS
    near_part, far_part = blocks * KEY_VALUE_HEADS // 2, KEY_VALUE_HEADS // 2

    def near_at(ref, half):
        return ref.at[pl.ds(half * near_part, near_part)]

    def far_at(ref, half, base=0):
        return ref.at[pl.ds(base + half * far_part, far_part)]

    def both(copies):
        return [copies(half) for half in range(2)]

    near_direct = both(lambda h: put(near_at(kv, h), near_at(near, h), near_send.at[h], near_recv.at[h], me + 1))
    far_direct = both(lambda h: put(far_at(kv, h, last), far_at(far, h), far_send.at[h], far_recv.at[h], me + 2))
    if relays:
        core, x, z = me % 2, me // 2 % 2, me // 4
        rows_z = window // 4
        to_relay = [(me - 2, relay_a), (me + 4, relay_b)]
        near_out = both(lambda h: put(near_at(kv, h), to_relay[h][1], relay_send.at[h], relay_recv.at[h], to_relay[h][0]))
        far_out = both(
            lambda h: put(
                far_at(kv, h, last), far_at(to_relay[h][1], 0), relay_send.at[h], relay_recv.at[h], to_relay[h][0]
            )
        )
        near_targets, far_targets = (me + 3, me - 3), (me + 4, me - 2)
        relay_refs = (relay_a, relay_b)
        near_on = both(
            lambda h: put(relay_refs[h], near_at(near, h), forward_send.at[h], near_recv.at[h], near_targets[h])
        )
        far_on = both(
            lambda h: put(far_at(relay_refs[h], 0), far_at(far, h), forward_send.at[h], far_recv.at[h], far_targets[h])
        )
        beside_far = both(lambda h: put(far_at(relay_b, h), far_at(far, h), chip_send.at[h], far_recv.at[h], me - 2))
        now = [
            ((x == 1) & (core == 1) & (z < rows_z - 1), near_out),
            ((x == 1) & (core == 0) & (z < rows_z - 1), far_out),
            ((core == 1) & (x == 0), near_direct),
            (x == 0, far_direct),
            (core == 0, near_direct),
        ]
        as_relay = [((x == 0) & (z < rows_z - 1)), ((x == 1) & (z > 0))]
    else:
        now = [(me + 1 < window, near_direct), (me + 2 < window, far_direct)]

    for condition, copies in now:

        @pl.when(condition)
        def _(copies=copies):
            for copy in copies:
                copy.start()

    def await_request(source, carry):
        asked(source).wait_recv()
        return carry

    lax.fori_loop(me + 1, window, await_request, 0)
    to_scalars = pltpu.make_async_copy(requests, scalars, scalar_sem)
    to_scalars.start()
    to_scalars.wait()

    def answer(other, at, slot):
        return pltpu.make_async_remote_copy(
            src_ref=answers.at[at], dst_ref=landed.at[slot], send_sem=answer_send.at[at], recv_sem=answer_recv.at[slot],
            device_id={"ctx": other},
        )

    def start_answer(j, carry):
        other = flip(me, window - 1 - j, window)

        @pl.when(other > me)
        def _():
            for c in range(cap):
                answers[other, c] = kv[scalars[other, 0, me * cap + c]]
            answer(other, other, me).start()

        return carry

    ahead = 2 if relays else window - 1
    lax.fori_loop(0, ahead, start_answer, 0)

    if relays:
        for half in range(2):
            for at_core, arriving, on in ((1, near_out, near_on), (0, far_out, far_on)):

                @pl.when(as_relay[half] & (core == at_core))
                def _(half=half, at_core=at_core, arriving=arriving, on=on):
                    arriving[half].wait_recv()
                    on[half].start()
                    if half == 1 and at_core == 1:
                        for copy in beside_far:
                            copy.start()

        lax.fori_loop(ahead, window - 1, start_answer, 0)

    to_users = pltpu.make_async_copy(users, user_scalars, scalar_sem)
    to_users.start()
    to_users.wait()

    @pl.when(me >= 1)
    def _():
        for copy in near_direct:
            copy.wait_recv()

    @pl.when(me >= 2)
    def _():
        for copy in far_direct:
            copy.wait_recv()

    width = LOCAL_BAND_SIZE * BLOCK_TOKENS
    factor = HEAD_SIZE**-0.5 * log2_e
    key = lax.broadcasted_iota(jnp.int32, (width, BLOCK_TOKENS), 0)
    query = lax.broadcasted_iota(jnp.int32, (width, BLOCK_TOKENS), 1)

    def store(h):
        return [
            pltpu.make_async_copy(partial_held.at[h], partial.at[h], store_sem.at[0, h]),
            pltpu.make_async_copy(stats_held.at[h], stats.at[h], store_sem.at[1, h]),
        ]

    def one_head(h, carry):
        load(h).wait()
        band = [far[h]] + [near[i * KEY_VALUE_HEADS + h] for i in range(blocks)]
        band = band + [kv[i * KEY_VALUE_HEADS + h] for i in range(blocks)]
        k_all = jnp.concatenate([b[0] for b in band], 0)
        v_all = with_ones(jnp.concatenate([b[1] for b in band], 1))
        for i in range(blocks):
            start = (me * blocks + i - (LOCAL_BAND_SIZE - 1)) * BLOCK_TOKENS
            good = (key <= query + (LOCAL_BAND_SIZE - 1) * BLOCK_TOKENS) & (key + start >= 0)
            bias = jnp.concatenate([jnp.where(good, 0.0, masked_score)] * CHUNK, 1)
            rows = slice(i * BLOCK_TOKENS, (i + 1) * BLOCK_TOKENS)
            k = k_all[i * BLOCK_TOKENS : i * BLOCK_TOKENS + width]
            v = v_all[:, i * BLOCK_TOKENS : i * BLOCK_TOKENS + width]
            q_cosine, q_sine = cosine[rows] * factor, sine[rows] * factor
            for part in range(GROUP // CHUNK):
                here = slice(part * CHUNK * BLOCK_TOKENS, (part + 1) * CHUNK * BLOCK_TOKENS)
                heads = range(part * CHUNK, (part + 1) * CHUNK)
                q = jnp.concatenate(
                    [rotate(q_held[h, rows, n * HEAD_SIZE : (n + 1) * HEAD_SIZE], q_cosine, q_sine) for n in heads], 0
                ).astype(jnp.bfloat16)
                rotated[i * KEY_VALUE_HEADS + h, here] = q
                score = dot_nt(k, q) + bias
                top = jnp.max(score, 0, keepdims=True)
                weight = jnp.exp2(score - top).astype(jnp.bfloat16)
                summed = jnp.dot(v, weight, preferred_element_type=jnp.float32)
                total = summed[HEAD_SIZE : HEAD_SIZE + 1]
                partial_held[h, i, :, here] = (summed[:HEAD_SIZE] * (1.0 / total)).astype(jnp.bfloat16)
                stats_held[h, i, :, here] = top + jnp.log2(total)
        for copy in store(h):
            copy.start()
        return carry

    lax.fori_loop(0, KEY_VALUE_HEADS, one_head, 0)

    def store_slots(source, side):
        place = pl.ds(source * cap, cap)
        return [
            pltpu.make_async_copy(slot_partial_held.at[side], slot_partial.at[place], slot_sem.at[0, side]),
            pltpu.make_async_copy(slot_stats_held.at[side], slot_stats.at[place], slot_sem.at[1, side]),
        ]

    def one_source(source, carry):
        side = source % 2
        answer(source, source, source).wait_recv()

        @pl.when(source >= 2)
        def _():
            for copy in store_slots(source - 2, side):
                copy.wait()

        for c in range(cap):
            k = landed[source, c, 0]
            v = with_ones(landed[source, c, 1])
            q = rotated[user_scalars[0, source * cap + c]]
            score = dot_nt(k, q)
            top = jnp.max(score, 0, keepdims=True)
            weight = jnp.exp2(score - top).astype(jnp.bfloat16)
            summed = jnp.dot(v, weight, preferred_element_type=jnp.float32)
            total = summed[HEAD_SIZE : HEAD_SIZE + 1]
            slot_partial_held[side, c] = (summed[:HEAD_SIZE] * (1.0 / total)).astype(jnp.bfloat16)
            slot_stats_held[side, c] = top + jnp.log2(total)
        for copy in store_slots(source, side):
            copy.start()
        return carry

    lax.fori_loop(0, me, one_source, 0)

    def end_slots(source, carry):
        for copy in store_slots(source, source % 2):
            copy.wait()
        return carry

    lax.fori_loop(jnp.maximum(me - 2, 0), me, end_slots, 0)

    def end_store(h, carry):
        for copy in store(h):
            copy.wait()
        return carry

    lax.fori_loop(0, KEY_VALUE_HEADS, end_store, 0)

    for condition, copies in now:

        @pl.when(condition)
        def _(copies=copies):
            for copy in copies:
                copy.wait_send()

    if relays:
        for half in range(2):
            for at_core, on in ((1, near_on), (0, far_on)):

                @pl.when(as_relay[half] & (core == at_core))
                def _(half=half, on=on):
                    on[half].wait_send()

        @pl.when(as_relay[1] & (core == 1))
        def _():
            for copy in beside_far:
                copy.wait_send()

    def end_ask(owner, carry):
        ask(owner).wait_send()
        return carry

    lax.fori_loop(0, me, end_ask, 0)

    def end_answer(other, carry):
        answer(other, other, me).wait_send()
        return carry

    lax.fori_loop(me + 1, window, end_answer, 0)


def merge_kernel(blocks, slots, partial, stats, *rest):
    slot_count = blocks * PICKED_BLOCKS
    slot_partials, slot_stats, out = rest[:slot_count], rest[slot_count:-1], rest[-1]
    head = pl.program_id(0)
    for i in range(blocks):
        alive = slots[0, (i * KEY_VALUE_HEADS + head) * PICKED_BLOCKS] >= 0
        rows = slice(i * BLOCK_TOKENS, (i + 1) * BLOCK_TOKENS)
        pair = range(i * PICKED_BLOCKS, (i + 1) * PICKED_BLOCKS)

        def give(part, result):
            for n in range(CHUNK):
                at = (part * CHUNK + n) * HEAD_SIZE
                out[rows, at : at + HEAD_SIZE] = result[:, n * BLOCK_TOKENS : (n + 1) * BLOCK_TOKENS].T.astype(jnp.bfloat16)

        @pl.when(alive)
        def _():
            for part in range(GROUP // CHUNK):
                here = slice(part * CHUNK * BLOCK_TOKENS, (part + 1) * CHUNK * BLOCK_TOKENS)
                logs = [stats[0, i, :, here]] + [slot_stats[p][0, :, here] for p in pair]
                terms = [partial[0, i, :, here]] + [slot_partials[p][0, :, here] for p in pair]
                top = functools.reduce(jnp.maximum, logs)
                weights = [jnp.exp2(log - top) for log in logs]
                inverse = 1.0 / sum(weights)
                give(part, sum(t.astype(jnp.float32) * (w * inverse) for t, w in zip(terms, weights)))

        @pl.when(jnp.logical_not(alive))
        def _():
            for part in range(GROUP // CHUNK):
                here = slice(part * CHUNK * BLOCK_TOKENS, (part + 1) * CHUNK * BLOCK_TOKENS)
                give(part, partial[0, i, :, here].astype(jnp.float32))


def shards(queries, keys, values, positions, picks):
    tokens = queries.shape[0]
    blocks = tokens // BLOCK_TOKENS
    window = lax.axis_size("ctx")
    cap = max(1, blocks * KEY_VALUE_HEADS * PICKED_BLOCKS // window)
    per_head = GROUP * HEAD_SIZE
    entries = blocks * KEY_VALUE_HEADS
    count = entries * PICKED_BLOCKS
    lanes = -(-window * cap // 128) * 128

    half = HEAD_SIZE // 2
    freq = rope_base ** (-(jnp.arange(half, dtype=jnp.float32) * 2.0) / HEAD_SIZE)
    angle = positions.astype(jnp.float32)[:, None] * freq[None, :]
    cosine, sine = jnp.cos(angle), jnp.sin(angle)
    cosine = jnp.concatenate([cosine, cosine], 1)
    sine = jnp.concatenate([-sine, sine], 1)

    here = pl.BlockSpec(memory_space=pltpu.VMEM)
    there = pl.BlockSpec(memory_space=pl.ANY)
    by_head = (KEY_VALUE_HEADS, tokens, per_head)
    stacked = GROUP * BLOCK_TOKENS
    slot_count = window * cap
    partial_dims = (KEY_VALUE_HEADS, blocks, HEAD_SIZE, stacked)
    stats_dims = (KEY_VALUE_HEADS, blocks, 1, stacked)
    width = LOCAL_BAND_SIZE * BLOCK_TOKENS
    limit = 56 * 1024 * 1024
    partial, stats, slot_partial, slot_stats, slots = pl.pallas_call(
        functools.partial(exchange_kernel, blocks, window, cap, window == 16),
        in_specs=[there] + [here] * 5,
        out_specs=[there] * 4 + [here],
        out_shape=[
            jax.ShapeDtypeStruct(partial_dims, jnp.bfloat16),
            jax.ShapeDtypeStruct(stats_dims, jnp.float32),
            jax.ShapeDtypeStruct((slot_count, HEAD_SIZE, stacked), jnp.bfloat16),
            jax.ShapeDtypeStruct((slot_count, 1, stacked), jnp.float32),
            jax.ShapeDtypeStruct((1, count), jnp.int32),
        ],
        scratch_shapes=[
            pltpu.VMEM(by_head, jnp.bfloat16),
            pltpu.VMEM((entries, stacked, HEAD_SIZE), jnp.bfloat16),
            pltpu.VMEM(partial_dims, jnp.bfloat16),
            pltpu.VMEM(stats_dims, jnp.float32),
            pltpu.VMEM((2, cap, HEAD_SIZE, stacked), jnp.bfloat16),
            pltpu.VMEM((2, cap, 1, stacked), jnp.float32),
            pltpu.VMEM((window, cap) + ENTRY, jnp.bfloat16),
            pltpu.VMEM((entries,) + ENTRY, jnp.bfloat16),
            pltpu.VMEM((entries,) + ENTRY, jnp.bfloat16),
            pltpu.VMEM((KEY_VALUE_HEADS,) + ENTRY, jnp.bfloat16),
            pltpu.VMEM((entries // 2,) + ENTRY, jnp.bfloat16),
            pltpu.VMEM((entries // 2,) + ENTRY, jnp.bfloat16),
            pltpu.VMEM((window, cap) + ENTRY, jnp.bfloat16),
            pltpu.VMEM((1, lanes), jnp.int32),
            pltpu.VMEM((window, 1, lanes), jnp.int32),
            pltpu.SMEM((window, 1, lanes), jnp.int32),
            pltpu.VMEM((1, lanes), jnp.int32),
            pltpu.SMEM((1, lanes), jnp.int32),
            pltpu.SemaphoreType.DMA((KEY_VALUE_HEADS,)),
            pltpu.SemaphoreType.DMA((2, KEY_VALUE_HEADS)),
            pltpu.SemaphoreType.DMA((2,)),
            pltpu.SemaphoreType.DMA((2,)),
            pltpu.SemaphoreType.DMA((2,)),
            pltpu.SemaphoreType.DMA((2,)),
            pltpu.SemaphoreType.DMA((2,)),
            pltpu.SemaphoreType.DMA((2,)),
            pltpu.SemaphoreType.DMA((2,)),
            pltpu.SemaphoreType.DMA((2,)),
            pltpu.SemaphoreType.DMA((window,)),
            pltpu.SemaphoreType.DMA((window,)),
            pltpu.SemaphoreType.DMA,
            pltpu.SemaphoreType.DMA((2, 2)),
            pltpu.SemaphoreType.DMA((window,)),
            pltpu.SemaphoreType.DMA((window,)),
        ],
        compiler_params=pltpu.CompilerParams(collective_id=0, has_side_effects=True, vmem_limit_bytes=limit),
        cost_estimate=pl.CostEstimate(
            flops=4 * tokens * QUERY_HEADS * HEAD_SIZE * width,
            bytes_accessed=tokens * QUERY_HEADS * HEAD_SIZE * 6,
            transcendentals=tokens * QUERY_HEADS * width,
        ),
        name="exchange_and_band",
    )(queries, keys, values, cosine, sine, picks.reshape(1, count))

    def slot_specs(dims):
        def spec(at):
            def place(h, slot):
                i, p = at // PICKED_BLOCKS, at % PICKED_BLOCKS
                return (jnp.maximum(slot[0, (i * KEY_VALUE_HEADS + h) * PICKED_BLOCKS + p], 0), 0, 0)

            return pl.BlockSpec((1,) + dims, place)

        return [spec(at) for at in range(blocks * PICKED_BLOCKS)]

    def head_spec(dims):
        return pl.BlockSpec((1,) + dims[1:], lambda h, *_: (h, 0, 0, 0))

    copies = blocks * PICKED_BLOCKS
    return pl.pallas_call(
        functools.partial(merge_kernel, blocks),
        grid_spec=pltpu.PrefetchScalarGridSpec(
            num_scalar_prefetch=1,
            grid=(KEY_VALUE_HEADS,),
            in_specs=[head_spec(partial_dims), head_spec(stats_dims)]
            + slot_specs((HEAD_SIZE, stacked))
            + slot_specs((1, stacked)),
            out_specs=pl.BlockSpec((tokens, per_head), lambda h, *_: (0, h)),
        ),
        out_shape=jax.ShapeDtypeStruct(queries.shape, jnp.bfloat16),
        compiler_params=pltpu.CompilerParams(vmem_limit_bytes=limit),
        name="merge",
    )(slots, partial, stats, *[slot_partial] * copies, *[slot_stats] * copies)


def solution(mesh):
    rows = P(("groups", "ctx"), None)
    return jax.shard_map(
        shards,
        mesh=mesh,
        in_specs=(rows, rows, rows, P(("groups", "ctx")), P(("groups", "ctx"), None, None)),
        out_specs=rows,
        check_vma=False,
    )
```

```python
import functools

import jax
import jax.numpy as jnp
from jax import lax
from jax.experimental import pallas as pl
from jax.experimental.pallas import tpu as pltpu
from jax.sharding import PartitionSpec as P

QUERY_HEADS = 64
KEY_VALUE_HEADS = 8
HEAD_SIZE = 128
BLOCK_TOKENS = 128
LOCAL_BAND_SIZE = 4
PICKED_BLOCKS = 2
GROUP = QUERY_HEADS // KEY_VALUE_HEADS
ENTRY = (2, BLOCK_TOKENS, HEAD_SIZE)

rope_base = 500000.0
masked_score = -1e30
log2_e = 1.4426950408889634


def rotate(x, cosine, sine):
    wide = x.astype(jnp.float32)
    return wide * cosine + pltpu.roll(wide, HEAD_SIZE // 2, 1) * sine


def dot_nt(a, b):
    return lax.dot_general(a, b, (((1,), (1,)), ((), ())), preferred_element_type=jnp.float32)


def with_ones(v):
    return jnp.concatenate([v, jnp.ones((16, v.shape[1]), v.dtype)], 0)


CHUNK = 4


def flip(a, b, size):
    out, bit = 0, 1
    while bit < size:
        out = out + (a // bit + b // bit) % 2 * bit
        bit *= 2
    return out


def exchange_kernel(
    blocks, window, cap, relays,
    queries, keys, values, cosine, sine, pick_row,
    partial, stats, slot_partial, slot_stats, slots,
    q_held, rotated, partial_held, stats_held, slot_partial_held, slot_stats_held, landed, kv, near, far, relay_a, relay_b, answers, request, requests, scalars, users, user_scalars,
    load_sem, store_sem, near_send, near_recv, far_send, far_recv, relay_send, relay_recv, forward_send, chip_send, request_send, request_recv, scalar_sem, slot_sem, answer_send, answer_recv,
):
    me = lax.axis_index("ctx")
    count = pick_row.shape[1]
    per_head = GROUP * HEAD_SIZE
    barrier = pltpu.get_barrier_semaphore()

    def greet(j, carry):
        pl.semaphore_signal(barrier, inc=1, device_id={"ctx": lax.rem(me + j, window)})
        return carry

    lax.fori_loop(1, window, greet, 0)

    def load(h):
        columns = pl.ds(pl.multiple_of(h * per_head, per_head), per_head)
        return pltpu.make_async_copy(queries.at[:, columns], q_held.at[h], load_sem.at[h])

    def start_load(h, carry):
        load(h).start()
        return carry

    lax.fori_loop(0, KEY_VALUE_HEADS, start_load, 0)

    row = pick_row[...]
    first = lax.broadcasted_iota(jnp.int32, (count, count), 0)
    second = lax.broadcasted_iota(jnp.int32, (count, count), 1)
    column = jnp.sum(jnp.where(first == second, row, 0), 1, keepdims=True)
    row_owner = jnp.maximum(row, 0) // blocks
    column_owner = jnp.maximum(column, 0) // blocks
    alike = (column_owner == row_owner) & (column >= 0) & (row >= 0)
    column_rank = jnp.sum((alike & (second < first)).astype(jnp.int32), 1, keepdims=True)
    row_rank = jnp.sum((alike & (first < second)).astype(jnp.int32), 0, keepdims=True)
    slots[...] = jnp.where(row >= 0, row_owner * cap + jnp.minimum(row_rank, cap - 1), -1)
    order = lax.broadcasted_iota(jnp.int32, (count, 1), 0)
    entry = jnp.maximum(column, 0) % blocks * KEY_VALUE_HEADS + order // PICKED_BLOCKS % KEY_VALUE_HEADS
    lane = lax.broadcasted_iota(jnp.int32, (count, request.shape[1]), 1)
    hit = (column_owner * cap + column_rank == lane) & (column >= 0)
    request[...] = jnp.sum(jnp.where(hit, entry, 0), 0, keepdims=True)
    users[...] = jnp.sum(jnp.where(hit, order // PICKED_BLOCKS, 0), 0, keepdims=True)

    for i in range(blocks):
        rows = slice(i * BLOCK_TOKENS, (i + 1) * BLOCK_TOKENS)
        for head in range(KEY_VALUE_HEADS):
            columns = slice(head * HEAD_SIZE, (head + 1) * HEAD_SIZE)
            kv[i * KEY_VALUE_HEADS + head, 0] = rotate(keys[rows, columns], cosine[rows], sine[rows]).astype(jnp.bfloat16)
            kv[i * KEY_VALUE_HEADS + head, 1] = values[rows, columns].astype(jnp.float32).T.astype(jnp.bfloat16)

    @pl.when(me < 1)
    def _():
        near[...] = jnp.zeros_like(near)

    @pl.when(me < 2)
    def _():
        far[...] = jnp.zeros_like(far)

    pl.semaphore_wait(barrier, window - 1)

    def ask(owner):
        return pltpu.make_async_remote_copy(
            src_ref=request, dst_ref=requests.at[me], send_sem=request_send.at[owner], recv_sem=request_recv.at[me],
            device_id={"ctx": owner},
        )

    def asked(source):
        return pltpu.make_async_remote_copy(
            src_ref=request, dst_ref=requests.at[source], send_sem=request_send.at[source],
            recv_sem=request_recv.at[source], device_id={"ctx": source},
        )

    def start_ask(owner, carry):
        ask(owner).start()
        return carry

    lax.fori_loop(0, me, start_ask, 0)

    def put(source, target, send_sem, recv_sem, to):
        return pltpu.make_async_remote_copy(
            src_ref=source, dst_ref=target, send_sem=send_sem, recv_sem=recv_sem,
            device_id={"ctx": lax.rem(to + window, window)},
        )

    last = (blocks - 1) * KEY_VALUE_HEADS
    near_part, far_part = blocks * KEY_VALUE_HEADS // 2, KEY_VALUE_HEADS // 2

    def near_at(ref, half):
        return ref.at[pl.ds(half * near_part, near_part)]

    def far_at(ref, half, base=0):
        return ref.at[pl.ds(base + half * far_part, far_part)]

    def both(copies):
        return [copies(half) for half in range(2)]

    near_direct = both(lambda h: put(near_at(kv, h), near_at(near, h), near_send.at[h], near_recv.at[h], me + 1))
    far_direct = both(lambda h: put(far_at(kv, h, last), far_at(far, h), far_send.at[h], far_recv.at[h], me + 2))
    if relays:
        core, x, z = me % 2, me // 2 % 2, me // 4
        rows_z = window // 4
        to_relay = [(me - 2, relay_a), (me + 4, relay_b)]
        near_out = both(lambda h: put(near_at(kv, h), to_relay[h][1], relay_send.at[h], relay_recv.at[h], to_relay[h][0]))
        far_out = both(
            lambda h: put(
                far_at(kv, h, last), far_at(to_relay[h][1], 0), relay_send.at[h], relay_recv.at[h], to_relay[h][0]
            )
        )
        near_targets, far_targets = (me + 3, me - 3), (me + 4, me - 2)
        relay_refs = (relay_a, relay_b)
        near_on = both(
            lambda h: put(relay_refs[h], near_at(near, h), forward_send.at[h], near_recv.at[h], near_targets[h])
        )
        far_on = both(
            lambda h: put(far_at(relay_refs[h], 0), far_at(far, h), forward_send.at[h], far_recv.at[h], far_targets[h])
        )
        beside_far = both(lambda h: put(far_at(relay_b, h), far_at(far, h), chip_send.at[h], far_recv.at[h], me - 2))
        now = [
            ((x == 1) & (core == 1) & (z < rows_z - 1), near_out),
            ((x == 1) & (core == 0) & (z < rows_z - 1), far_out),
            ((core == 1) & (x == 0), near_direct),
            (x == 0, far_direct),
            (core == 0, near_direct),
        ]
        as_relay = [((x == 0) & (z < rows_z - 1)), ((x == 1) & (z > 0))]
    else:
        now = [(me + 1 < window, near_direct), (me + 2 < window, far_direct)]

    for condition, copies in now:

        @pl.when(condition)
        def _(copies=copies):
            for copy in copies:
                copy.start()

    def await_request(source, carry):
        asked(source).wait_recv()
        return carry

    lax.fori_loop(me + 1, window, await_request, 0)
    to_scalars = pltpu.make_async_copy(requests, scalars, scalar_sem)
    to_scalars.start()
    to_scalars.wait()

    def answer(other, at, slot):
        return pltpu.make_async_remote_copy(
            src_ref=answers.at[at], dst_ref=landed.at[slot], send_sem=answer_send.at[at], recv_sem=answer_recv.at[slot],
            device_id={"ctx": other},
        )

    def gather_answer(other, carry):
        for c in range(cap):
            answers[other, c] = kv[scalars[other, 0, me * cap + c]]
        return carry

    lax.fori_loop(me + 1, window, gather_answer, 0)

    def start_answer(j, carry):
        other = flip(me, window - 1 - j, window)

        @pl.when(other > me)
        def _():
            answer(other, other, me).start()

        return carry

    if relays:
        for half in range(2):
            for at_core, arriving, on in ((1, near_out, near_on), (0, far_out, far_on)):

                @pl.when(as_relay[half] & (core == at_core))
                def _(half=half, at_core=at_core, arriving=arriving, on=on):
                    arriving[half].wait_recv()
                    on[half].start()
                    if half == 1 and at_core == 1:
                        for copy in beside_far:
                            copy.start()

    lax.fori_loop(0, window - 1, start_answer, 0)

    to_users = pltpu.make_async_copy(users, user_scalars, scalar_sem)
    to_users.start()
    to_users.wait()

    @pl.when(me >= 1)
    def _():
        for copy in near_direct:
            copy.wait_recv()

    @pl.when(me >= 2)
    def _():
        for copy in far_direct:
            copy.wait_recv()

    width = LOCAL_BAND_SIZE * BLOCK_TOKENS
    factor = HEAD_SIZE**-0.5 * log2_e
    key = lax.broadcasted_iota(jnp.int32, (width, BLOCK_TOKENS), 0)
    query = lax.broadcasted_iota(jnp.int32, (width, BLOCK_TOKENS), 1)

    def store(h):
        return [
            pltpu.make_async_copy(partial_held.at[h], partial.at[h], store_sem.at[0, h]),
            pltpu.make_async_copy(stats_held.at[h], stats.at[h], store_sem.at[1, h]),
        ]

    def one_head(h, carry):
        load(h).wait()
        band = [far[h]] + [near[i * KEY_VALUE_HEADS + h] for i in range(blocks)]
        band = band + [kv[i * KEY_VALUE_HEADS + h] for i in range(blocks)]
        k_all = jnp.concatenate([b[0] for b in band], 0)
        v_all = with_ones(jnp.concatenate([b[1] for b in band], 1))
        for i in range(blocks):
            start = (me * blocks + i - (LOCAL_BAND_SIZE - 1)) * BLOCK_TOKENS
            good = (key <= query + (LOCAL_BAND_SIZE - 1) * BLOCK_TOKENS) & (key + start >= 0)
            bias = jnp.concatenate([jnp.where(good, 0.0, masked_score)] * CHUNK, 1)
            rows = slice(i * BLOCK_TOKENS, (i + 1) * BLOCK_TOKENS)
            k = k_all[i * BLOCK_TOKENS : i * BLOCK_TOKENS + width]
            v = v_all[:, i * BLOCK_TOKENS : i * BLOCK_TOKENS + width]
            q_cosine, q_sine = cosine[rows] * factor, sine[rows] * factor
            for part in range(GROUP // CHUNK):
                here = slice(part * CHUNK * BLOCK_TOKENS, (part + 1) * CHUNK * BLOCK_TOKENS)
                heads = range(part * CHUNK, (part + 1) * CHUNK)
                q = jnp.concatenate(
                    [rotate(q_held[h, rows, n * HEAD_SIZE : (n + 1) * HEAD_SIZE], q_cosine, q_sine) for n in heads], 0
                ).astype(jnp.bfloat16)
                rotated[i * KEY_VALUE_HEADS + h, here] = q
                score = dot_nt(k, q) + bias
                top = jnp.max(score, 0, keepdims=True)
                weight = jnp.exp2(score - top).astype(jnp.bfloat16)
                summed = jnp.dot(v, weight, preferred_element_type=jnp.float32)
                total = summed[HEAD_SIZE : HEAD_SIZE + 1]
                partial_held[h, i, :, here] = (summed[:HEAD_SIZE] * (1.0 / total)).astype(jnp.bfloat16)
                stats_held[h, i, :, here] = top + jnp.log2(total)
        for copy in store(h):
            copy.start()
        return carry

    lax.fori_loop(0, KEY_VALUE_HEADS, one_head, 0)

    def store_slots(source, side):
        place = pl.ds(source * cap, cap)
        return [
            pltpu.make_async_copy(slot_partial_held.at[side], slot_partial.at[place], slot_sem.at[0, side]),
            pltpu.make_async_copy(slot_stats_held.at[side], slot_stats.at[place], slot_sem.at[1, side]),
        ]

    def one_source(j, done):
        source = flip(me, window - 1 - j, window)
        side = done % 2

        @pl.when(source < me)
        def _():
            answer(source, source, source).wait_recv()

            @pl.when(done >= 2)
            def _():
                for copy in store_slots(source, side):
                    copy.wait()

            for c in range(cap):
                k = landed[source, c, 0]
                v = with_ones(landed[source, c, 1])
                q = rotated[user_scalars[0, source * cap + c]]
                score = dot_nt(k, q)
                top = jnp.max(score, 0, keepdims=True)
                weight = jnp.exp2(score - top).astype(jnp.bfloat16)
                summed = jnp.dot(v, weight, preferred_element_type=jnp.float32)
                total = summed[HEAD_SIZE : HEAD_SIZE + 1]
                slot_partial_held[side, c] = (summed[:HEAD_SIZE] * (1.0 / total)).astype(jnp.bfloat16)
                slot_stats_held[side, c] = top + jnp.log2(total)
            for copy in store_slots(source, side):
                copy.start()

        return done + jnp.where(source < me, 1, 0)

    lax.fori_loop(0, window - 1, one_source, jnp.int32(0))

    def end_slots(source, carry):
        for copy in store_slots(source, source % 2):
            copy.wait()
        return carry

    lax.fori_loop(jnp.maximum(me - 2, 0), me, end_slots, 0)

    def end_store(h, carry):
        for copy in store(h):
            copy.wait()
        return carry

    lax.fori_loop(0, KEY_VALUE_HEADS, end_store, 0)

    for condition, copies in now:

        @pl.when(condition)
        def _(copies=copies):
            for copy in copies:
                copy.wait_send()

    if relays:
        for half in range(2):
            for at_core, on in ((1, near_on), (0, far_on)):

                @pl.when(as_relay[half] & (core == at_core))
                def _(half=half, on=on):
                    on[half].wait_send()

        @pl.when(as_relay[1] & (core == 1))
        def _():
            for copy in beside_far:
                copy.wait_send()

    def end_ask(owner, carry):
        ask(owner).wait_send()
        return carry

    lax.fori_loop(0, me, end_ask, 0)

    def end_answer(other, carry):
        answer(other, other, me).wait_send()
        return carry

    lax.fori_loop(me + 1, window, end_answer, 0)


def merge_kernel(blocks, slots, partial, stats, *rest):
    slot_count = blocks * PICKED_BLOCKS
    slot_partials, slot_stats, out = rest[:slot_count], rest[slot_count:-1], rest[-1]
    head = pl.program_id(0)
    row = lax.broadcasted_iota(jnp.int32, (BLOCK_TOKENS, BLOCK_TOKENS), 0)
    column = lax.broadcasted_iota(jnp.int32, (BLOCK_TOKENS, BLOCK_TOKENS), 1)
    identity = jnp.where(row == column, 1.0, 0.0).astype(jnp.bfloat16)
    for i in range(blocks):
        alive = slots[0, (i * KEY_VALUE_HEADS + head) * PICKED_BLOCKS] >= 0
        rows = slice(i * BLOCK_TOKENS, (i + 1) * BLOCK_TOKENS)
        pair = range(i * PICKED_BLOCKS, (i + 1) * PICKED_BLOCKS)

        def give(part, result):
            for n in range(CHUNK):
                at = (part * CHUNK + n) * HEAD_SIZE
                turned = dot_nt(identity, result[:, n * BLOCK_TOKENS : (n + 1) * BLOCK_TOKENS].astype(jnp.bfloat16))
                out[rows, at : at + HEAD_SIZE] = turned.astype(jnp.bfloat16)

        @pl.when(alive)
        def _():
            for part in range(GROUP // CHUNK):
                here = slice(part * CHUNK * BLOCK_TOKENS, (part + 1) * CHUNK * BLOCK_TOKENS)
                logs = [stats[0, i, :, here]] + [slot_stats[p][0, :, here] for p in pair]
                terms = [partial[0, i, :, here]] + [slot_partials[p][0, :, here] for p in pair]
                top = functools.reduce(jnp.maximum, logs)
                weights = [jnp.exp2(log - top) for log in logs]
                inverse = 1.0 / sum(weights)
                give(part, sum(t.astype(jnp.float32) * (w * inverse) for t, w in zip(terms, weights)))

        @pl.when(jnp.logical_not(alive))
        def _():
            for part in range(GROUP // CHUNK):
                here = slice(part * CHUNK * BLOCK_TOKENS, (part + 1) * CHUNK * BLOCK_TOKENS)
                give(part, partial[0, i, :, here].astype(jnp.float32))


def shards(queries, keys, values, positions, picks):
    tokens = queries.shape[0]
    blocks = tokens // BLOCK_TOKENS
    window = lax.axis_size("ctx")
    cap = max(1, blocks * KEY_VALUE_HEADS * PICKED_BLOCKS // window)
    per_head = GROUP * HEAD_SIZE
    entries = blocks * KEY_VALUE_HEADS
    count = entries * PICKED_BLOCKS
    lanes = -(-window * cap // 128) * 128

    half = HEAD_SIZE // 2
    freq = rope_base ** (-(jnp.arange(half, dtype=jnp.float32) * 2.0) / HEAD_SIZE)
    angle = positions.astype(jnp.float32)[:, None] * freq[None, :]
    cosine, sine = jnp.cos(angle), jnp.sin(angle)
    cosine = jnp.concatenate([cosine, cosine], 1)
    sine = jnp.concatenate([-sine, sine], 1)

    here = pl.BlockSpec(memory_space=pltpu.VMEM)
    there = pl.BlockSpec(memory_space=pl.ANY)
    by_head = (KEY_VALUE_HEADS, tokens, per_head)
    stacked = GROUP * BLOCK_TOKENS
    slot_count = window * cap
    partial_dims = (KEY_VALUE_HEADS, blocks, HEAD_SIZE, stacked)
    stats_dims = (KEY_VALUE_HEADS, blocks, 1, stacked)
    width = LOCAL_BAND_SIZE * BLOCK_TOKENS
    limit = 56 * 1024 * 1024
    partial, stats, slot_partial, slot_stats, slots = pl.pallas_call(
        functools.partial(exchange_kernel, blocks, window, cap, window == 16),
        in_specs=[there] + [here] * 5,
        out_specs=[there] * 4 + [here],
        out_shape=[
            jax.ShapeDtypeStruct(partial_dims, jnp.bfloat16),
            jax.ShapeDtypeStruct(stats_dims, jnp.float32),
            jax.ShapeDtypeStruct((slot_count, HEAD_SIZE, stacked), jnp.bfloat16),
            jax.ShapeDtypeStruct((slot_count, 1, stacked), jnp.float32),
            jax.ShapeDtypeStruct((1, count), jnp.int32),
        ],
        scratch_shapes=[
            pltpu.VMEM(by_head, jnp.bfloat16),
            pltpu.VMEM((entries, stacked, HEAD_SIZE), jnp.bfloat16),
            pltpu.VMEM(partial_dims, jnp.bfloat16),
            pltpu.VMEM(stats_dims, jnp.float32),
            pltpu.VMEM((2, cap, HEAD_SIZE, stacked), jnp.bfloat16),
            pltpu.VMEM((2, cap, 1, stacked), jnp.float32),
            pltpu.VMEM((window, cap) + ENTRY, jnp.bfloat16),
            pltpu.VMEM((entries,) + ENTRY, jnp.bfloat16),
            pltpu.VMEM((entries,) + ENTRY, jnp.bfloat16),
            pltpu.VMEM((KEY_VALUE_HEADS,) + ENTRY, jnp.bfloat16),
            pltpu.VMEM((entries // 2,) + ENTRY, jnp.bfloat16),
            pltpu.VMEM((entries // 2,) + ENTRY, jnp.bfloat16),
            pltpu.VMEM((window, cap) + ENTRY, jnp.bfloat16),
            pltpu.VMEM((1, lanes), jnp.int32),
            pltpu.VMEM((window, 1, lanes), jnp.int32),
            pltpu.SMEM((window, 1, lanes), jnp.int32),
            pltpu.VMEM((1, lanes), jnp.int32),
            pltpu.SMEM((1, lanes), jnp.int32),
            pltpu.SemaphoreType.DMA((KEY_VALUE_HEADS,)),
            pltpu.SemaphoreType.DMA((2, KEY_VALUE_HEADS)),
            pltpu.SemaphoreType.DMA((2,)),
            pltpu.SemaphoreType.DMA((2,)),
            pltpu.SemaphoreType.DMA((2,)),
            pltpu.SemaphoreType.DMA((2,)),
            pltpu.SemaphoreType.DMA((2,)),
            pltpu.SemaphoreType.DMA((2,)),
            pltpu.SemaphoreType.DMA((2,)),
            pltpu.SemaphoreType.DMA((2,)),
            pltpu.SemaphoreType.DMA((window,)),
            pltpu.SemaphoreType.DMA((window,)),
            pltpu.SemaphoreType.DMA,
            pltpu.SemaphoreType.DMA((2, 2)),
            pltpu.SemaphoreType.DMA((window,)),
            pltpu.SemaphoreType.DMA((window,)),
        ],
        compiler_params=pltpu.CompilerParams(collective_id=0, has_side_effects=True, vmem_limit_bytes=limit),
        cost_estimate=pl.CostEstimate(
            flops=4 * tokens * QUERY_HEADS * HEAD_SIZE * width,
            bytes_accessed=tokens * QUERY_HEADS * HEAD_SIZE * 6,
            transcendentals=tokens * QUERY_HEADS * width,
        ),
        name="exchange_and_band",
    )(queries, keys, values, cosine, sine, picks.reshape(1, count))

    def slot_specs(dims):
        def spec(at):
            def place(h, slot):
                i, p = at // PICKED_BLOCKS, at % PICKED_BLOCKS
                return (jnp.maximum(slot[0, (i * KEY_VALUE_HEADS + h) * PICKED_BLOCKS + p], 0), 0, 0)

            return pl.BlockSpec((1,) + dims, place)

        return [spec(at) for at in range(blocks * PICKED_BLOCKS)]

    def head_spec(dims):
        return pl.BlockSpec((1,) + dims[1:], lambda h, *_: (h, 0, 0, 0))

    copies = blocks * PICKED_BLOCKS
    return pl.pallas_call(
        functools.partial(merge_kernel, blocks),
        grid_spec=pltpu.PrefetchScalarGridSpec(
            num_scalar_prefetch=1,
            grid=(KEY_VALUE_HEADS,),
            in_specs=[head_spec(partial_dims), head_spec(stats_dims)]
            + slot_specs((HEAD_SIZE, stacked))
            + slot_specs((1, stacked)),
            out_specs=pl.BlockSpec((tokens, per_head), lambda h, *_: (0, h)),
        ),
        out_shape=jax.ShapeDtypeStruct(queries.shape, jnp.bfloat16),
        compiler_params=pltpu.CompilerParams(vmem_limit_bytes=limit),
        name="merge",
    )(slots, partial, stats, *[slot_partial] * copies, *[slot_stats] * copies)


def solution(mesh):
    rows = P(("groups", "ctx"), None)
    return jax.shard_map(
        shards,
        mesh=mesh,
        in_specs=(rows, rows, rows, P(("groups", "ctx")), P(("groups", "ctx"), None, None)),
        out_specs=rows,
        check_vma=False,
    )
```

```python
import functools

import jax
import jax.numpy as jnp
from jax import lax
from jax.experimental import pallas as pl
from jax.experimental.pallas import tpu as pltpu
from jax.sharding import PartitionSpec as P

QUERY_HEADS = 64
KEY_VALUE_HEADS = 8
HEAD_SIZE = 128
BLOCK_TOKENS = 128
LOCAL_BAND_SIZE = 4
PICKED_BLOCKS = 2
GROUP = QUERY_HEADS // KEY_VALUE_HEADS
ENTRY = (2, BLOCK_TOKENS, HEAD_SIZE)

rope_base = 500000.0
masked_score = -1e30
log2_e = 1.4426950408889634


def rotate(x, cosine, sine):
    wide = x.astype(jnp.float32)
    return wide * cosine + pltpu.roll(wide, HEAD_SIZE // 2, 1) * sine


def dot_nt(a, b):
    return lax.dot_general(a, b, (((1,), (1,)), ((), ())), preferred_element_type=jnp.float32)


def with_ones(v):
    return jnp.concatenate([v, jnp.ones((16, v.shape[1]), v.dtype)], 0)


CHUNK = 4


def flip(a, b, size):
    out, bit = 0, 1
    while bit < size:
        out = out + (a // bit + b // bit) % 2 * bit
        bit *= 2
    return out


def exchange_kernel(
    blocks, window, cap, relays,
    queries, keys, values, cosine, sine, pick_row,
    partial, stats, slot_partial, slot_stats, slots,
    q_held, rotated, partial_held, stats_held, slot_partial_held, slot_stats_held, landed, kv, near, far, relay_a, relay_b, answers, request, requests, scalars, users, user_scalars,
    load_sem, store_sem, near_send, near_recv, far_send, far_recv, relay_send, relay_recv, forward_send, chip_send, request_send, request_recv, scalar_sem, slot_sem, answer_send, answer_recv,
):
    me = lax.axis_index("ctx")
    count = pick_row.shape[1]
    per_head = GROUP * HEAD_SIZE
    barrier = pltpu.get_barrier_semaphore()

    def greet(j, carry):
        pl.semaphore_signal(barrier, inc=1, device_id={"ctx": lax.rem(me + j, window)})
        return carry

    lax.fori_loop(1, window, greet, 0)

    def load(h):
        columns = pl.ds(pl.multiple_of(h * per_head, per_head), per_head)
        return pltpu.make_async_copy(queries.at[:, columns], q_held.at[h], load_sem.at[h])

    def start_load(h, carry):
        load(h).start()
        return carry

    lax.fori_loop(0, KEY_VALUE_HEADS, start_load, 0)

    row = pick_row[...]
    first = lax.broadcasted_iota(jnp.int32, (count, count), 0)
    second = lax.broadcasted_iota(jnp.int32, (count, count), 1)
    column = jnp.sum(jnp.where(first == second, row, 0), 1, keepdims=True)
    row_owner = jnp.maximum(row, 0) // blocks
    column_owner = jnp.maximum(column, 0) // blocks
    alike = (column_owner == row_owner) & (column >= 0) & (row >= 0)
    column_rank = jnp.sum((alike & (second < first)).astype(jnp.int32), 1, keepdims=True)
    row_rank = jnp.sum((alike & (first < second)).astype(jnp.int32), 0, keepdims=True)
    slots[...] = jnp.where(row >= 0, row_owner * cap + jnp.minimum(row_rank, cap - 1), -1)
    order = lax.broadcasted_iota(jnp.int32, (count, 1), 0)
    entry = jnp.maximum(column, 0) % blocks * KEY_VALUE_HEADS + order // PICKED_BLOCKS % KEY_VALUE_HEADS
    lane = lax.broadcasted_iota(jnp.int32, (count, request.shape[1]), 1)
    hit = (column_owner * cap + column_rank == lane) & (column >= 0)
    request[...] = jnp.sum(jnp.where(hit, entry, 0), 0, keepdims=True)
    users[...] = jnp.sum(jnp.where(hit, order // PICKED_BLOCKS, 0), 0, keepdims=True)

    for i in range(blocks):
        rows = slice(i * BLOCK_TOKENS, (i + 1) * BLOCK_TOKENS)
        for head in range(KEY_VALUE_HEADS):
            columns = slice(head * HEAD_SIZE, (head + 1) * HEAD_SIZE)
            kv[i * KEY_VALUE_HEADS + head, 0] = rotate(keys[rows, columns], cosine[rows], sine[rows]).astype(jnp.bfloat16)
            kv[i * KEY_VALUE_HEADS + head, 1] = values[rows, columns].astype(jnp.float32).T.astype(jnp.bfloat16)

    @pl.when(me < 1)
    def _():
        near[...] = jnp.zeros_like(near)

    @pl.when(me < 2)
    def _():
        far[...] = jnp.zeros_like(far)

    pl.semaphore_wait(barrier, window - 1)

    def ask(owner):
        return pltpu.make_async_remote_copy(
            src_ref=request, dst_ref=requests.at[me], send_sem=request_send.at[owner], recv_sem=request_recv.at[me],
            device_id={"ctx": owner},
        )

    def asked(source):
        return pltpu.make_async_remote_copy(
            src_ref=request, dst_ref=requests.at[source], send_sem=request_send.at[source],
            recv_sem=request_recv.at[source], device_id={"ctx": source},
        )

    def start_ask(owner, carry):
        ask(owner).start()
        return carry

    lax.fori_loop(0, me, start_ask, 0)

    def put(source, target, send_sem, recv_sem, to):
        return pltpu.make_async_remote_copy(
            src_ref=source, dst_ref=target, send_sem=send_sem, recv_sem=recv_sem,
            device_id={"ctx": lax.rem(to + window, window)},
        )

    last = (blocks - 1) * KEY_VALUE_HEADS
    near_part, far_part = blocks * KEY_VALUE_HEADS // 2, KEY_VALUE_HEADS // 2

    def near_at(ref, half):
        return ref.at[pl.ds(half * near_part, near_part)]

    def far_at(ref, half, base=0):
        return ref.at[pl.ds(base + half * far_part, far_part)]

    def both(copies):
        return [copies(half) for half in range(2)]

    near_direct = both(lambda h: put(near_at(kv, h), near_at(near, h), near_send.at[h], near_recv.at[h], me + 1))
    far_direct = both(lambda h: put(far_at(kv, h, last), far_at(far, h), far_send.at[h], far_recv.at[h], me + 2))
    if relays:
        core, x, z = me % 2, me // 2 % 2, me // 4
        rows_z = window // 4
        to_relay = [(me - 2, relay_a), (me + 4, relay_b)]
        near_out = both(lambda h: put(near_at(kv, h), to_relay[h][1], relay_send.at[h], relay_recv.at[h], to_relay[h][0]))
        far_out = both(
            lambda h: put(
                far_at(kv, h, last), far_at(to_relay[h][1], 0), relay_send.at[h], relay_recv.at[h], to_relay[h][0]
            )
        )
        near_targets, far_targets = (me + 3, me - 3), (me + 4, me - 2)
        relay_refs = (relay_a, relay_b)
        near_on = both(
            lambda h: put(relay_refs[h], near_at(near, h), forward_send.at[h], near_recv.at[h], near_targets[h])
        )
        far_on = both(
            lambda h: put(far_at(relay_refs[h], 0), far_at(far, h), forward_send.at[h], far_recv.at[h], far_targets[h])
        )
        beside_far = both(lambda h: put(far_at(relay_b, h), far_at(far, h), chip_send.at[h], far_recv.at[h], me - 2))
        now = [
            ((x == 1) & (core == 1) & (z < rows_z - 1), near_out),
            ((x == 1) & (core == 0) & (z < rows_z - 1), far_out),
            ((core == 1) & (x == 0), near_direct),
            ((core == 0) & (x == 0), far_direct),
            (core == 0, near_direct),
        ]
        as_relay = [((x == 0) & (z < rows_z - 1)), ((x == 1) & (z > 0))]
    else:
        now = [(me + 1 < window, near_direct), (me + 2 < window, far_direct)]

    for condition, copies in now:

        @pl.when(condition)
        def _(copies=copies):
            for copy in copies:
                copy.start()

    def await_request(source, carry):
        asked(source).wait_recv()
        return carry

    lax.fori_loop(me + 1, window, await_request, 0)
    to_scalars = pltpu.make_async_copy(requests, scalars, scalar_sem)
    to_scalars.start()
    to_scalars.wait()

    def answer(other, at, slot):
        return pltpu.make_async_remote_copy(
            src_ref=answers.at[at], dst_ref=landed.at[slot], send_sem=answer_send.at[at], recv_sem=answer_recv.at[slot],
            device_id={"ctx": other},
        )

    def start_answer(j, carry):
        other = flip(me, window - 1 - j, window)

        @pl.when(other > me)
        def _():
            for c in range(cap):
                answers[other, c] = kv[scalars[other, 0, me * cap + c]]
            answer(other, other, me).start()

        return carry

    ahead = 2
    lax.fori_loop(0, ahead, start_answer, 0)

    if relays:
        for half in range(2):
            for at_core, arriving, on in ((1, near_out, near_on), (0, far_out, far_on)):

                @pl.when(as_relay[half] & (core == at_core))
                def _(half=half, at_core=at_core, arriving=arriving, on=on):
                    arriving[half].wait_recv()
                    on[half].start()
                    if half == 1 and at_core == 1:
                        for copy in beside_far:
                            copy.start()

        @pl.when((core == 1) & (x == 0))
        def _():
            for copy in far_direct:
                copy.start()

    lax.fori_loop(ahead, window - 1, start_answer, 0)

    to_users = pltpu.make_async_copy(users, user_scalars, scalar_sem)
    to_users.start()
    to_users.wait()

    @pl.when(me >= 1)
    def _():
        for copy in near_direct:
            copy.wait_recv()

    @pl.when(me >= 2)
    def _():
        for copy in far_direct:
            copy.wait_recv()

    width = LOCAL_BAND_SIZE * BLOCK_TOKENS
    factor = HEAD_SIZE**-0.5 * log2_e
    key = lax.broadcasted_iota(jnp.int32, (width, BLOCK_TOKENS), 0)
    query = lax.broadcasted_iota(jnp.int32, (width, BLOCK_TOKENS), 1)

    def store(h):
        return [
            pltpu.make_async_copy(partial_held.at[h], partial.at[h], store_sem.at[0, h]),
            pltpu.make_async_copy(stats_held.at[h], stats.at[h], store_sem.at[1, h]),
        ]

    def one_head(h, carry):
        load(h).wait()
        band = [far[h]] + [near[i * KEY_VALUE_HEADS + h] for i in range(blocks)]
        band = band + [kv[i * KEY_VALUE_HEADS + h] for i in range(blocks)]
        k_all = jnp.concatenate([b[0] for b in band], 0)
        v_all = with_ones(jnp.concatenate([b[1] for b in band], 1))
        for i in range(blocks):
            start = (me * blocks + i - (LOCAL_BAND_SIZE - 1)) * BLOCK_TOKENS
            good = (key <= query + (LOCAL_BAND_SIZE - 1) * BLOCK_TOKENS) & (key + start >= 0)
            bias = jnp.concatenate([jnp.where(good, 0.0, masked_score)] * CHUNK, 1)
            rows = slice(i * BLOCK_TOKENS, (i + 1) * BLOCK_TOKENS)
            k = k_all[i * BLOCK_TOKENS : i * BLOCK_TOKENS + width]
            v = v_all[:, i * BLOCK_TOKENS : i * BLOCK_TOKENS + width]
            q_cosine, q_sine = cosine[rows] * factor, sine[rows] * factor
            for part in range(GROUP // CHUNK):
                here = slice(part * CHUNK * BLOCK_TOKENS, (part + 1) * CHUNK * BLOCK_TOKENS)
                heads = range(part * CHUNK, (part + 1) * CHUNK)
                q = jnp.concatenate(
                    [rotate(q_held[h, rows, n * HEAD_SIZE : (n + 1) * HEAD_SIZE], q_cosine, q_sine) for n in heads], 0
                ).astype(jnp.bfloat16)
                rotated[i * KEY_VALUE_HEADS + h, here] = q
                score = dot_nt(k, q) + bias
                top = jnp.max(score, 0, keepdims=True)
                weight = jnp.exp2(score - top).astype(jnp.bfloat16)
                summed = jnp.dot(v, weight, preferred_element_type=jnp.float32)
                total = summed[HEAD_SIZE : HEAD_SIZE + 1]
                partial_held[h, i, :, here] = (summed[:HEAD_SIZE] * (1.0 / total)).astype(jnp.bfloat16)
                stats_held[h, i, :, here] = top + jnp.log2(total)
        for copy in store(h):
            copy.start()
        return carry

    lax.fori_loop(0, KEY_VALUE_HEADS, one_head, 0)

    def store_slots(source, side):
        place = pl.ds(source * cap, cap)
        return [
            pltpu.make_async_copy(slot_partial_held.at[side], slot_partial.at[place], slot_sem.at[0, side]),
            pltpu.make_async_copy(slot_stats_held.at[side], slot_stats.at[place], slot_sem.at[1, side]),
        ]

    def one_source(j, done):
        source = flip(me, window - 1 - j, window)
        side = done % 2

        @pl.when(source < me)
        def _():
            answer(source, source, source).wait_recv()

            @pl.when(done >= 2)
            def _():
                for copy in store_slots(source, side):
                    copy.wait()

            for c in range(cap):
                k = landed[source, c, 0]
                v = with_ones(landed[source, c, 1])
                q = rotated[user_scalars[0, source * cap + c]]
                score = dot_nt(k, q)
                top = jnp.max(score, 0, keepdims=True)
                weight = jnp.exp2(score - top).astype(jnp.bfloat16)
                summed = jnp.dot(v, weight, preferred_element_type=jnp.float32)
                total = summed[HEAD_SIZE : HEAD_SIZE + 1]
                slot_partial_held[side, c] = (summed[:HEAD_SIZE] * (1.0 / total)).astype(jnp.bfloat16)
                slot_stats_held[side, c] = top + jnp.log2(total)
            for copy in store_slots(source, side):
                copy.start()

        return done + jnp.where(source < me, 1, 0)

    lax.fori_loop(0, window - 1, one_source, jnp.int32(0))

    def end_slots(source, carry):
        for copy in store_slots(source, source % 2):
            copy.wait()
        return carry

    lax.fori_loop(jnp.maximum(me - 2, 0), me, end_slots, 0)

    def end_store(h, carry):
        for copy in store(h):
            copy.wait()
        return carry

    lax.fori_loop(0, KEY_VALUE_HEADS, end_store, 0)

    for condition, copies in now:

        @pl.when(condition)
        def _(copies=copies):
            for copy in copies:
                copy.wait_send()

    if relays:
        for half in range(2):
            for at_core, on in ((1, near_on), (0, far_on)):

                @pl.when(as_relay[half] & (core == at_core))
                def _(half=half, on=on):
                    on[half].wait_send()

        @pl.when(as_relay[1] & (core == 1))
        def _():
            for copy in beside_far:
                copy.wait_send()

        @pl.when((core == 1) & (x == 0))
        def _():
            for copy in far_direct:
                copy.wait_send()

    def end_ask(owner, carry):
        ask(owner).wait_send()
        return carry

    lax.fori_loop(0, me, end_ask, 0)

    def end_answer(other, carry):
        answer(other, other, me).wait_send()
        return carry

    lax.fori_loop(me + 1, window, end_answer, 0)


def merge_kernel(
    blocks, slots, partial, stats, slot_partial, slot_stats, out,
    partial_held, stats_held, slot_partial_held, slot_stats_held, out_held, load_sem, slot_sem, stats_sem, store_sem,
):
    ahead = 3
    per_head = out_held.shape[2]

    def first_pick(h, i):
        return (i * KEY_VALUE_HEADS + h) * PICKED_BLOCKS

    def load(h):
        return pltpu.make_async_copy(partial.at[h], partial_held.at[h], load_sem.at[h])

    def load_slot(at):
        slot = jnp.maximum(slots[0, at], 0)
        return pltpu.make_async_copy(slot_partial.at[slot], slot_partial_held.at[at], slot_sem.at[at])

    def store(h):
        columns = pl.ds(pl.multiple_of(h * per_head, per_head), per_head)
        return pltpu.make_async_copy(out_held.at[h], out.at[:, columns], store_sem.at[h])

    def start(h, carry):
        load(h).start()
        for i in range(blocks):
            at = first_pick(h, i)

            @pl.when(slots[0, at] >= 0)
            def _():
                for p in range(PICKED_BLOCKS):
                    load_slot(at + p).start()

        return carry

    all_stats = [
        pltpu.make_async_copy(stats, stats_held, stats_sem.at[0]),
        pltpu.make_async_copy(slot_stats, slot_stats_held, stats_sem.at[1]),
    ]
    for copy in all_stats:
        copy.start()
    lax.fori_loop(0, ahead, start, 0)
    for copy in all_stats:
        copy.wait()

    def one_head(h, carry):
        @pl.when(h + ahead < KEY_VALUE_HEADS)
        def _():
            start(h + ahead, 0)

        load(h).wait()
        for i in range(blocks):
            at = first_pick(h, i)
            alive = slots[0, at] >= 0
            rows = slice(i * BLOCK_TOKENS, (i + 1) * BLOCK_TOKENS)

            def give(part, result):
                for n in range(CHUNK):
                    place = (part * CHUNK + n) * HEAD_SIZE
                    turned = result[:, n * BLOCK_TOKENS : (n + 1) * BLOCK_TOKENS].T
                    out_held[h, rows, place : place + HEAD_SIZE] = turned.astype(jnp.bfloat16)

            @pl.when(alive)
            def _():
                for p in range(PICKED_BLOCKS):
                    load_slot(at + p).wait()
                for part in range(GROUP // CHUNK):
                    here = slice(part * CHUNK * BLOCK_TOKENS, (part + 1) * CHUNK * BLOCK_TOKENS)
                    logs = [stats_held[h, i, :, here]]
                    terms = [partial_held[h, i, :, here]]
                    for p in range(PICKED_BLOCKS):
                        logs.append(slot_stats_held[slots[0, at + p], :, here])
                        terms.append(slot_partial_held[at + p, :, here])
                    top = functools.reduce(jnp.maximum, logs)
                    weights = [jnp.exp2(log - top) for log in logs]
                    inverse = 1.0 / sum(weights)
                    give(part, sum(t.astype(jnp.float32) * (w * inverse) for t, w in zip(terms, weights)))

            @pl.when(jnp.logical_not(alive))
            def _():
                for part in range(GROUP // CHUNK):
                    here = slice(part * CHUNK * BLOCK_TOKENS, (part + 1) * CHUNK * BLOCK_TOKENS)
                    give(part, partial_held[h, i, :, here].astype(jnp.float32))

        store(h).start()
        return carry

    lax.fori_loop(0, KEY_VALUE_HEADS, one_head, 0)

    def end_store(h, carry):
        store(h).wait()
        return carry

    lax.fori_loop(0, KEY_VALUE_HEADS, end_store, 0)


def shards(queries, keys, values, positions, picks):
    tokens = queries.shape[0]
    blocks = tokens // BLOCK_TOKENS
    window = lax.axis_size("ctx")
    cap = max(1, blocks * KEY_VALUE_HEADS * PICKED_BLOCKS // window)
    per_head = GROUP * HEAD_SIZE
    entries = blocks * KEY_VALUE_HEADS
    count = entries * PICKED_BLOCKS
    lanes = -(-window * cap // 128) * 128

    half = HEAD_SIZE // 2
    freq = rope_base ** (-(jnp.arange(half, dtype=jnp.float32) * 2.0) / HEAD_SIZE)
    angle = positions.astype(jnp.float32)[:, None] * freq[None, :]
    cosine, sine = jnp.cos(angle), jnp.sin(angle)
    cosine = jnp.concatenate([cosine, cosine], 1)
    sine = jnp.concatenate([-sine, sine], 1)

    here = pl.BlockSpec(memory_space=pltpu.VMEM)
    there = pl.BlockSpec(memory_space=pl.ANY)
    by_head = (KEY_VALUE_HEADS, tokens, per_head)
    stacked = GROUP * BLOCK_TOKENS
    slot_count = window * cap
    partial_dims = (KEY_VALUE_HEADS, blocks, HEAD_SIZE, stacked)
    stats_dims = (KEY_VALUE_HEADS, blocks, 1, stacked)
    width = LOCAL_BAND_SIZE * BLOCK_TOKENS
    limit = 56 * 1024 * 1024
    partial, stats, slot_partial, slot_stats, slots = pl.pallas_call(
        functools.partial(exchange_kernel, blocks, window, cap, window == 16),
        in_specs=[there] + [here] * 5,
        out_specs=[there] * 4 + [here],
        out_shape=[
            jax.ShapeDtypeStruct(partial_dims, jnp.bfloat16),
            jax.ShapeDtypeStruct(stats_dims, jnp.float32),
            jax.ShapeDtypeStruct((slot_count, HEAD_SIZE, stacked), jnp.bfloat16),
            jax.ShapeDtypeStruct((slot_count, 1, stacked), jnp.float32),
            jax.ShapeDtypeStruct((1, count), jnp.int32),
        ],
        scratch_shapes=[
            pltpu.VMEM(by_head, jnp.bfloat16),
            pltpu.VMEM((entries, stacked, HEAD_SIZE), jnp.bfloat16),
            pltpu.VMEM(partial_dims, jnp.bfloat16),
            pltpu.VMEM(stats_dims, jnp.float32),
            pltpu.VMEM((2, cap, HEAD_SIZE, stacked), jnp.bfloat16),
            pltpu.VMEM((2, cap, 1, stacked), jnp.float32),
            pltpu.VMEM((window, cap) + ENTRY, jnp.bfloat16),
            pltpu.VMEM((entries,) + ENTRY, jnp.bfloat16),
            pltpu.VMEM((entries,) + ENTRY, jnp.bfloat16),
            pltpu.VMEM((KEY_VALUE_HEADS,) + ENTRY, jnp.bfloat16),
            pltpu.VMEM((entries // 2,) + ENTRY, jnp.bfloat16),
            pltpu.VMEM((entries // 2,) + ENTRY, jnp.bfloat16),
            pltpu.VMEM((window, cap) + ENTRY, jnp.bfloat16),
            pltpu.VMEM((1, lanes), jnp.int32),
            pltpu.VMEM((window, 1, lanes), jnp.int32),
            pltpu.SMEM((window, 1, lanes), jnp.int32),
            pltpu.VMEM((1, lanes), jnp.int32),
            pltpu.SMEM((1, lanes), jnp.int32),
            pltpu.SemaphoreType.DMA((KEY_VALUE_HEADS,)),
            pltpu.SemaphoreType.DMA((2, KEY_VALUE_HEADS)),
            pltpu.SemaphoreType.DMA((2,)),
            pltpu.SemaphoreType.DMA((2,)),
            pltpu.SemaphoreType.DMA((2,)),
            pltpu.SemaphoreType.DMA((2,)),
            pltpu.SemaphoreType.DMA((2,)),
            pltpu.SemaphoreType.DMA((2,)),
            pltpu.SemaphoreType.DMA((2,)),
            pltpu.SemaphoreType.DMA((2,)),
            pltpu.SemaphoreType.DMA((window,)),
            pltpu.SemaphoreType.DMA((window,)),
            pltpu.SemaphoreType.DMA,
            pltpu.SemaphoreType.DMA((2, 2)),
            pltpu.SemaphoreType.DMA((window,)),
            pltpu.SemaphoreType.DMA((window,)),
        ],
        compiler_params=pltpu.CompilerParams(collective_id=0, has_side_effects=True, vmem_limit_bytes=limit),
        cost_estimate=pl.CostEstimate(
            flops=4 * tokens * QUERY_HEADS * HEAD_SIZE * width,
            bytes_accessed=tokens * QUERY_HEADS * HEAD_SIZE * 6,
            transcendentals=tokens * QUERY_HEADS * width,
        ),
        name="exchange_and_band",
    )(queries, keys, values, cosine, sine, picks.reshape(1, count))

    return pl.pallas_call(
        functools.partial(merge_kernel, blocks),
        in_specs=[pl.BlockSpec(memory_space=pltpu.SMEM)] + [there] * 4,
        out_specs=there,
        out_shape=jax.ShapeDtypeStruct(queries.shape, jnp.bfloat16),
        scratch_shapes=[
            pltpu.VMEM(partial_dims, jnp.bfloat16),
            pltpu.VMEM(stats_dims, jnp.float32),
            pltpu.VMEM((count, HEAD_SIZE, stacked), jnp.bfloat16),
            pltpu.VMEM((slot_count, 1, stacked), jnp.float32),
            pltpu.VMEM(by_head, jnp.bfloat16),
            pltpu.SemaphoreType.DMA((KEY_VALUE_HEADS,)),
            pltpu.SemaphoreType.DMA((count,)),
            pltpu.SemaphoreType.DMA((2,)),
            pltpu.SemaphoreType.DMA((KEY_VALUE_HEADS,)),
        ],
        compiler_params=pltpu.CompilerParams(vmem_limit_bytes=limit),
        name="merge",
    )(slots, partial, stats, slot_partial, slot_stats)


def solution(mesh):
    rows = P(("groups", "ctx"), None)
    return jax.shard_map(
        shards,
        mesh=mesh,
        in_specs=(rows, rows, rows, P(("groups", "ctx")), P(("groups", "ctx"), None, None)),
        out_specs=rows,
        check_vma=False,
    )
```

```python
import functools

import jax
import jax.numpy as jnp
from jax import lax
from jax.experimental import pallas as pl
from jax.experimental.pallas import tpu as pltpu
from jax.sharding import PartitionSpec as P

QUERY_HEADS = 64
KEY_VALUE_HEADS = 8
HEAD_SIZE = 128
BLOCK_TOKENS = 128
LOCAL_BAND_SIZE = 4
PICKED_BLOCKS = 2
GROUP = QUERY_HEADS // KEY_VALUE_HEADS
ENTRY = (2, BLOCK_TOKENS, HEAD_SIZE)

rope_base = 500000.0
masked_score = -1e30
log2_e = 1.4426950408889634


def rotate(x, cosine, sine):
    wide = x.astype(jnp.float32)
    return wide * cosine + pltpu.roll(wide, HEAD_SIZE // 2, 1) * sine


def dot_nt(a, b):
    return lax.dot_general(a, b, (((1,), (1,)), ((), ())), preferred_element_type=jnp.float32)


def with_ones(v):
    return jnp.concatenate([v, jnp.ones((16, v.shape[1]), v.dtype)], 0)


CHUNK = 4


def flip(a, b, size):
    out, bit = 0, 1
    while bit < size:
        out = out + (a // bit + b // bit) % 2 * bit
        bit *= 2
    return out


def exchange_kernel(
    blocks, window, cap, relays,
    queries, keys, values, cosine, sine, pick_row,
    partial, stats, slot_partial, slot_stats, slots,
    q_held, rotated, partial_held, stats_held, slot_partial_held, slot_stats_held, landed, kv, near, far, relay_a, relay_b, answers, request, requests, scalars, users, user_scalars,
    load_sem, store_sem, near_send, near_recv, far_send, far_recv, relay_send, relay_recv, forward_send, chip_send, request_send, request_recv, scalar_sem, slot_sem, answer_send, answer_recv,
):
    me = lax.axis_index("ctx")
    count = pick_row.shape[1]
    per_head = GROUP * HEAD_SIZE
    barrier = pltpu.get_barrier_semaphore()

    def greet(j, carry):
        pl.semaphore_signal(barrier, inc=1, device_id={"ctx": lax.rem(me + j, window)})
        return carry

    lax.fori_loop(1, window, greet, 0)

    def load(h):
        columns = pl.ds(pl.multiple_of(h * per_head, per_head), per_head)
        return pltpu.make_async_copy(queries.at[:, columns], q_held.at[h], load_sem.at[h])

    def start_load(h, carry):
        load(h).start()
        return carry

    lax.fori_loop(0, KEY_VALUE_HEADS, start_load, 0)

    row = pick_row[...]
    first = lax.broadcasted_iota(jnp.int32, (count, count), 0)
    second = lax.broadcasted_iota(jnp.int32, (count, count), 1)
    column = jnp.sum(jnp.where(first == second, row, 0), 1, keepdims=True)
    row_owner = jnp.maximum(row, 0) // blocks
    column_owner = jnp.maximum(column, 0) // blocks
    alike = (column_owner == row_owner) & (column >= 0) & (row >= 0)
    column_rank = jnp.sum((alike & (second < first)).astype(jnp.int32), 1, keepdims=True)
    row_rank = jnp.sum((alike & (first < second)).astype(jnp.int32), 0, keepdims=True)
    slots[...] = jnp.where(row >= 0, row_owner * cap + jnp.minimum(row_rank, cap - 1), -1)
    order = lax.broadcasted_iota(jnp.int32, (count, 1), 0)
    entry = jnp.maximum(column, 0) % blocks * KEY_VALUE_HEADS + order // PICKED_BLOCKS % KEY_VALUE_HEADS
    lane = lax.broadcasted_iota(jnp.int32, (count, request.shape[1]), 1)
    hit = (column_owner * cap + column_rank == lane) & (column >= 0)
    request[...] = jnp.sum(jnp.where(hit, entry, 0), 0, keepdims=True)
    users[...] = jnp.sum(jnp.where(hit, order // PICKED_BLOCKS, 0), 0, keepdims=True)

    for i in range(blocks):
        rows = slice(i * BLOCK_TOKENS, (i + 1) * BLOCK_TOKENS)
        for head in range(KEY_VALUE_HEADS):
            columns = slice(head * HEAD_SIZE, (head + 1) * HEAD_SIZE)
            kv[i * KEY_VALUE_HEADS + head, 0] = rotate(keys[rows, columns], cosine[rows], sine[rows]).astype(jnp.bfloat16)
            kv[i * KEY_VALUE_HEADS + head, 1] = values[rows, columns].astype(jnp.float32).T.astype(jnp.bfloat16)

    @pl.when(me < 1)
    def _():
        near[...] = jnp.zeros_like(near)

    @pl.when(me < 2)
    def _():
        far[...] = jnp.zeros_like(far)

    pl.semaphore_wait(barrier, window - 1)

    def ask(owner):
        return pltpu.make_async_remote_copy(
            src_ref=request, dst_ref=requests.at[me], send_sem=request_send.at[owner], recv_sem=request_recv.at[me],
            device_id={"ctx": owner},
        )

    def asked(source):
        return pltpu.make_async_remote_copy(
            src_ref=request, dst_ref=requests.at[source], send_sem=request_send.at[source],
            recv_sem=request_recv.at[source], device_id={"ctx": source},
        )

    def start_ask(owner, carry):
        ask(owner).start()
        return carry

    lax.fori_loop(0, me, start_ask, 0)

    def put(source, target, send_sem, recv_sem, to):
        return pltpu.make_async_remote_copy(
            src_ref=source, dst_ref=target, send_sem=send_sem, recv_sem=recv_sem,
            device_id={"ctx": lax.rem(to + window, window)},
        )

    last = (blocks - 1) * KEY_VALUE_HEADS
    near_part, far_part = blocks * KEY_VALUE_HEADS // 2, KEY_VALUE_HEADS // 2

    def near_at(ref, half):
        return ref.at[pl.ds(half * near_part, near_part)]

    def far_at(ref, half, base=0):
        return ref.at[pl.ds(base + half * far_part, far_part)]

    def both(copies):
        return [copies(half) for half in range(2)]

    near_direct = both(lambda h: put(near_at(kv, h), near_at(near, h), near_send.at[h], near_recv.at[h], me + 1))
    far_direct = both(lambda h: put(far_at(kv, h, last), far_at(far, h), far_send.at[h], far_recv.at[h], me + 2))
    if relays:
        core, x, z = me % 2, me // 2 % 2, me // 4
        rows_z = window // 4
        to_relay = [(me - 2, relay_a), (me + 4, relay_b)]
        near_out = both(lambda h: put(near_at(kv, h), to_relay[h][1], relay_send.at[h], relay_recv.at[h], to_relay[h][0]))
        far_out = both(
            lambda h: put(
                far_at(kv, h, last), far_at(to_relay[h][1], 0), relay_send.at[h], relay_recv.at[h], to_relay[h][0]
            )
        )
        near_targets, far_targets = (me + 3, me - 3), (me + 4, me - 2)
        relay_refs = (relay_a, relay_b)
        near_on = both(
            lambda h: put(relay_refs[h], near_at(near, h), forward_send.at[h], near_recv.at[h], near_targets[h])
        )
        far_on = both(
            lambda h: put(far_at(relay_refs[h], 0), far_at(far, h), forward_send.at[h], far_recv.at[h], far_targets[h])
        )
        beside_far = both(lambda h: put(far_at(relay_b, h), far_at(far, h), chip_send.at[h], far_recv.at[h], me - 2))
        now = [
            ((x == 1) & (core == 1) & (z < rows_z - 1), near_out),
            ((x == 1) & (core == 0) & (z < rows_z - 1), far_out),
            ((core == 1) & (x == 0), near_direct),
            ((core == 0) & (x == 0), far_direct),
            (core == 0, near_direct),
        ]
        as_relay = [((x == 0) & (z < rows_z - 1)), ((x == 1) & (z > 0))]
    else:
        now = [(me + 1 < window, near_direct), (me + 2 < window, far_direct)]

    for condition, copies in now:

        @pl.when(condition)
        def _(copies=copies):
            for copy in copies:
                copy.start()

    def await_request(source, carry):
        asked(source).wait_recv()
        return carry

    lax.fori_loop(me + 1, window, await_request, 0)
    to_scalars = pltpu.make_async_copy(requests, scalars, scalar_sem)
    to_scalars.start()
    to_scalars.wait()

    def answer(other, at, slot):
        return pltpu.make_async_remote_copy(
            src_ref=answers.at[at], dst_ref=landed.at[slot], send_sem=answer_send.at[at], recv_sem=answer_recv.at[slot],
            device_id={"ctx": other},
        )

    def start_answer(j, carry):
        other = flip(me, window - 1 - j, window)

        @pl.when(other > me)
        def _():
            for c in range(cap):
                answers[other, c] = kv[scalars[other, 0, me * cap + c]]
            answer(other, other, me).start()

        return carry

    ahead = 1
    lax.fori_loop(0, ahead, start_answer, 0)

    if relays:
        for half in range(2):
            for at_core, arriving, on in ((1, near_out, near_on), (0, far_out, far_on)):

                @pl.when(as_relay[half] & (core == at_core))
                def _(half=half, at_core=at_core, arriving=arriving, on=on):
                    arriving[half].wait_recv()
                    on[half].start()
                    if half == 1 and at_core == 1:
                        for copy in beside_far:
                            copy.start()

        @pl.when((core == 1) & (x == 0))
        def _():
            for copy in far_direct:
                copy.start()

    lax.fori_loop(ahead, window - 1, start_answer, 0)

    to_users = pltpu.make_async_copy(users, user_scalars, scalar_sem)
    to_users.start()
    to_users.wait()

    width = LOCAL_BAND_SIZE * BLOCK_TOKENS
    factor = HEAD_SIZE**-0.5 * log2_e
    key = lax.broadcasted_iota(jnp.int32, (width, BLOCK_TOKENS), 0)
    query = lax.broadcasted_iota(jnp.int32, (width, BLOCK_TOKENS), 1)

    def store(h):
        return [
            pltpu.make_async_copy(partial_held.at[h], partial.at[h], store_sem.at[0, h]),
            pltpu.make_async_copy(stats_held.at[h], stats.at[h], store_sem.at[1, h]),
        ]

    def rotate_head(h, carry):
        load(h).wait()
        for i in range(blocks):
            rows = slice(i * BLOCK_TOKENS, (i + 1) * BLOCK_TOKENS)
            q_cosine, q_sine = cosine[rows] * factor, sine[rows] * factor
            for n in range(GROUP):
                q = rotate(q_held[h, rows, n * HEAD_SIZE : (n + 1) * HEAD_SIZE], q_cosine, q_sine)
                rotated[i * KEY_VALUE_HEADS + h, n * BLOCK_TOKENS : (n + 1) * BLOCK_TOKENS] = q.astype(jnp.bfloat16)
        return carry

    lax.fori_loop(0, KEY_VALUE_HEADS, rotate_head, 0)

    def store_slots(source, side):
        place = pl.ds(source * cap, cap)
        return [
            pltpu.make_async_copy(slot_partial_held.at[side], slot_partial.at[place], slot_sem.at[0, side]),
            pltpu.make_async_copy(slot_stats_held.at[side], slot_stats.at[place], slot_sem.at[1, side]),
        ]

    def one_source(j, done):
        source = flip(me, window - 1 - j, window)
        side = done % 2

        @pl.when(source < me)
        def _():
            answer(source, source, source).wait_recv()

            @pl.when(done >= 2)
            def _():
                for copy in store_slots(source, side):
                    copy.wait()

            for c in range(cap):
                k = landed[source, c, 0]
                v = with_ones(landed[source, c, 1])
                q = rotated[user_scalars[0, source * cap + c]]
                score = dot_nt(k, q)
                top = jnp.max(score, 0, keepdims=True)
                weight = jnp.exp2(score - top).astype(jnp.bfloat16)
                summed = jnp.dot(v, weight, preferred_element_type=jnp.float32)
                total = summed[HEAD_SIZE : HEAD_SIZE + 1]
                slot_partial_held[side, c] = (summed[:HEAD_SIZE] * (1.0 / total)).astype(jnp.bfloat16)
                slot_stats_held[side, c] = top + jnp.log2(total)
            for copy in store_slots(source, side):
                copy.start()

        return done + jnp.where(source < me, 1, 0)

    early = min(3, window - 1)
    done = lax.fori_loop(0, early, one_source, jnp.int32(0))

    @pl.when(me >= 1)
    def _():
        for copy in near_direct:
            copy.wait_recv()

    @pl.when(me >= 2)
    def _():
        for copy in far_direct:
            copy.wait_recv()

    def one_head(h, carry):
        band = [far[h]] + [near[i * KEY_VALUE_HEADS + h] for i in range(blocks)]
        band = band + [kv[i * KEY_VALUE_HEADS + h] for i in range(blocks)]
        k_all = jnp.concatenate([b[0] for b in band], 0)
        v_all = with_ones(jnp.concatenate([b[1] for b in band], 1))
        for i in range(blocks):
            start = (me * blocks + i - (LOCAL_BAND_SIZE - 1)) * BLOCK_TOKENS
            good = (key <= query + (LOCAL_BAND_SIZE - 1) * BLOCK_TOKENS) & (key + start >= 0)
            bias = jnp.concatenate([jnp.where(good, 0.0, masked_score)] * CHUNK, 1)
            k = k_all[i * BLOCK_TOKENS : i * BLOCK_TOKENS + width]
            v = v_all[:, i * BLOCK_TOKENS : i * BLOCK_TOKENS + width]
            for part in range(GROUP // CHUNK):
                here = slice(part * CHUNK * BLOCK_TOKENS, (part + 1) * CHUNK * BLOCK_TOKENS)
                q = rotated[i * KEY_VALUE_HEADS + h, here]
                score = dot_nt(k, q) + bias
                top = jnp.max(score, 0, keepdims=True)
                weight = jnp.exp2(score - top).astype(jnp.bfloat16)
                summed = jnp.dot(v, weight, preferred_element_type=jnp.float32)
                total = summed[HEAD_SIZE : HEAD_SIZE + 1]
                partial_held[h, i, :, here] = (summed[:HEAD_SIZE] * (1.0 / total)).astype(jnp.bfloat16)
                stats_held[h, i, :, here] = top + jnp.log2(total)
        for copy in store(h):
            copy.start()
        return carry

    lax.fori_loop(0, KEY_VALUE_HEADS, one_head, 0)

    lax.fori_loop(early, window - 1, one_source, done)

    def end_slots(source, carry):
        for copy in store_slots(source, source % 2):
            copy.wait()
        return carry

    lax.fori_loop(jnp.maximum(me - 2, 0), me, end_slots, 0)

    def end_store(h, carry):
        for copy in store(h):
            copy.wait()
        return carry

    lax.fori_loop(0, KEY_VALUE_HEADS, end_store, 0)

    for condition, copies in now:

        @pl.when(condition)
        def _(copies=copies):
            for copy in copies:
                copy.wait_send()

    if relays:
        for half in range(2):
            for at_core, on in ((1, near_on), (0, far_on)):

                @pl.when(as_relay[half] & (core == at_core))
                def _(half=half, on=on):
                    on[half].wait_send()

        @pl.when(as_relay[1] & (core == 1))
        def _():
            for copy in beside_far:
                copy.wait_send()

        @pl.when((core == 1) & (x == 0))
        def _():
            for copy in far_direct:
                copy.wait_send()

    def end_ask(owner, carry):
        ask(owner).wait_send()
        return carry

    lax.fori_loop(0, me, end_ask, 0)

    def end_answer(other, carry):
        answer(other, other, me).wait_send()
        return carry

    lax.fori_loop(me + 1, window, end_answer, 0)


def merge_kernel(
    blocks, slots, partial, stats, slot_partial, slot_stats, out,
    partial_held, stats_held, slot_partial_held, slot_stats_held, out_held, load_sem, slot_sem, stats_sem, store_sem,
):
    ahead = 3
    per_head = out_held.shape[2]

    def first_pick(h, i):
        return (i * KEY_VALUE_HEADS + h) * PICKED_BLOCKS

    def load(h):
        return pltpu.make_async_copy(partial.at[h], partial_held.at[h], load_sem.at[h])

    def load_slot(at):
        slot = jnp.maximum(slots[0, at], 0)
        return pltpu.make_async_copy(slot_partial.at[slot], slot_partial_held.at[at], slot_sem.at[at])

    def store(h):
        columns = pl.ds(pl.multiple_of(h * per_head, per_head), per_head)
        return pltpu.make_async_copy(out_held.at[h], out.at[:, columns], store_sem.at[h])

    def start(h, carry):
        load(h).start()
        for i in range(blocks):
            at = first_pick(h, i)

            @pl.when(slots[0, at] >= 0)
            def _():
                for p in range(PICKED_BLOCKS):
                    load_slot(at + p).start()

        return carry

    all_stats = [
        pltpu.make_async_copy(stats, stats_held, stats_sem.at[0]),
        pltpu.make_async_copy(slot_stats, slot_stats_held, stats_sem.at[1]),
    ]
    for copy in all_stats:
        copy.start()
    lax.fori_loop(0, ahead, start, 0)
    for copy in all_stats:
        copy.wait()

    def one_head(h, carry):
        @pl.when(h + ahead < KEY_VALUE_HEADS)
        def _():
            start(h + ahead, 0)

        load(h).wait()
        for i in range(blocks):
            at = first_pick(h, i)
            alive = slots[0, at] >= 0
            rows = slice(i * BLOCK_TOKENS, (i + 1) * BLOCK_TOKENS)

            def give(part, result):
                for n in range(CHUNK):
                    place = (part * CHUNK + n) * HEAD_SIZE
                    turned = result[:, n * BLOCK_TOKENS : (n + 1) * BLOCK_TOKENS].T
                    out_held[h, rows, place : place + HEAD_SIZE] = turned.astype(jnp.bfloat16)

            @pl.when(alive)
            def _():
                for p in range(PICKED_BLOCKS):
                    load_slot(at + p).wait()
                for part in range(GROUP // CHUNK):
                    here = slice(part * CHUNK * BLOCK_TOKENS, (part + 1) * CHUNK * BLOCK_TOKENS)
                    logs = [stats_held[h, i, :, here]]
                    terms = [partial_held[h, i, :, here]]
                    for p in range(PICKED_BLOCKS):
                        logs.append(slot_stats_held[slots[0, at + p], :, here])
                        terms.append(slot_partial_held[at + p, :, here])
                    top = functools.reduce(jnp.maximum, logs)
                    weights = [jnp.exp2(log - top) for log in logs]
                    inverse = 1.0 / sum(weights)
                    give(part, sum(t.astype(jnp.float32) * (w * inverse) for t, w in zip(terms, weights)))

            @pl.when(jnp.logical_not(alive))
            def _():
                for part in range(GROUP // CHUNK):
                    here = slice(part * CHUNK * BLOCK_TOKENS, (part + 1) * CHUNK * BLOCK_TOKENS)
                    give(part, partial_held[h, i, :, here].astype(jnp.float32))

        store(h).start()
        return carry

    lax.fori_loop(0, KEY_VALUE_HEADS, one_head, 0)

    def end_store(h, carry):
        store(h).wait()
        return carry

    lax.fori_loop(0, KEY_VALUE_HEADS, end_store, 0)


def shards(queries, keys, values, positions, picks):
    tokens = queries.shape[0]
    blocks = tokens // BLOCK_TOKENS
    window = lax.axis_size("ctx")
    cap = max(1, blocks * KEY_VALUE_HEADS * PICKED_BLOCKS // window)
    per_head = GROUP * HEAD_SIZE
    entries = blocks * KEY_VALUE_HEADS
    count = entries * PICKED_BLOCKS
    lanes = -(-window * cap // 128) * 128

    half = HEAD_SIZE // 2
    freq = rope_base ** (-(jnp.arange(half, dtype=jnp.float32) * 2.0) / HEAD_SIZE)
    angle = positions.astype(jnp.float32)[:, None] * freq[None, :]
    cosine, sine = jnp.cos(angle), jnp.sin(angle)
    cosine = jnp.concatenate([cosine, cosine], 1)
    sine = jnp.concatenate([-sine, sine], 1)

    here = pl.BlockSpec(memory_space=pltpu.VMEM)
    there = pl.BlockSpec(memory_space=pl.ANY)
    by_head = (KEY_VALUE_HEADS, tokens, per_head)
    stacked = GROUP * BLOCK_TOKENS
    slot_count = window * cap
    partial_dims = (KEY_VALUE_HEADS, blocks, HEAD_SIZE, stacked)
    stats_dims = (KEY_VALUE_HEADS, blocks, 1, stacked)
    width = LOCAL_BAND_SIZE * BLOCK_TOKENS
    limit = 56 * 1024 * 1024
    partial, stats, slot_partial, slot_stats, slots = pl.pallas_call(
        functools.partial(exchange_kernel, blocks, window, cap, window == 16),
        in_specs=[there] + [here] * 5,
        out_specs=[there] * 4 + [here],
        out_shape=[
            jax.ShapeDtypeStruct(partial_dims, jnp.bfloat16),
            jax.ShapeDtypeStruct(stats_dims, jnp.float32),
            jax.ShapeDtypeStruct((slot_count, HEAD_SIZE, stacked), jnp.bfloat16),
            jax.ShapeDtypeStruct((slot_count, 1, stacked), jnp.float32),
            jax.ShapeDtypeStruct((1, count), jnp.int32),
        ],
        scratch_shapes=[
            pltpu.VMEM(by_head, jnp.bfloat16),
            pltpu.VMEM((entries, stacked, HEAD_SIZE), jnp.bfloat16),
            pltpu.VMEM(partial_dims, jnp.bfloat16),
            pltpu.VMEM(stats_dims, jnp.float32),
            pltpu.VMEM((2, cap, HEAD_SIZE, stacked), jnp.bfloat16),
            pltpu.VMEM((2, cap, 1, stacked), jnp.float32),
            pltpu.VMEM((window, cap) + ENTRY, jnp.bfloat16),
            pltpu.VMEM((entries,) + ENTRY, jnp.bfloat16),
            pltpu.VMEM((entries,) + ENTRY, jnp.bfloat16),
            pltpu.VMEM((KEY_VALUE_HEADS,) + ENTRY, jnp.bfloat16),
            pltpu.VMEM((entries // 2,) + ENTRY, jnp.bfloat16),
            pltpu.VMEM((entries // 2,) + ENTRY, jnp.bfloat16),
            pltpu.VMEM((window, cap) + ENTRY, jnp.bfloat16),
            pltpu.VMEM((1, lanes), jnp.int32),
            pltpu.VMEM((window, 1, lanes), jnp.int32),
            pltpu.SMEM((window, 1, lanes), jnp.int32),
            pltpu.VMEM((1, lanes), jnp.int32),
            pltpu.SMEM((1, lanes), jnp.int32),
            pltpu.SemaphoreType.DMA((KEY_VALUE_HEADS,)),
            pltpu.SemaphoreType.DMA((2, KEY_VALUE_HEADS)),
            pltpu.SemaphoreType.DMA((2,)),
            pltpu.SemaphoreType.DMA((2,)),
            pltpu.SemaphoreType.DMA((2,)),
            pltpu.SemaphoreType.DMA((2,)),
            pltpu.SemaphoreType.DMA((2,)),
            pltpu.SemaphoreType.DMA((2,)),
            pltpu.SemaphoreType.DMA((2,)),
            pltpu.SemaphoreType.DMA((2,)),
            pltpu.SemaphoreType.DMA((window,)),
            pltpu.SemaphoreType.DMA((window,)),
            pltpu.SemaphoreType.DMA,
            pltpu.SemaphoreType.DMA((2, 2)),
            pltpu.SemaphoreType.DMA((window,)),
            pltpu.SemaphoreType.DMA((window,)),
        ],
        compiler_params=pltpu.CompilerParams(collective_id=0, has_side_effects=True, vmem_limit_bytes=limit),
        cost_estimate=pl.CostEstimate(
            flops=4 * tokens * QUERY_HEADS * HEAD_SIZE * width,
            bytes_accessed=tokens * QUERY_HEADS * HEAD_SIZE * 6,
            transcendentals=tokens * QUERY_HEADS * width,
        ),
        name="exchange_and_band",
    )(queries, keys, values, cosine, sine, picks.reshape(1, count))

    return pl.pallas_call(
        functools.partial(merge_kernel, blocks),
        in_specs=[pl.BlockSpec(memory_space=pltpu.SMEM)] + [there] * 4,
        out_specs=there,
        out_shape=jax.ShapeDtypeStruct(queries.shape, jnp.bfloat16),
        scratch_shapes=[
            pltpu.VMEM(partial_dims, jnp.bfloat16),
            pltpu.VMEM(stats_dims, jnp.float32),
            pltpu.VMEM((count, HEAD_SIZE, stacked), jnp.bfloat16),
            pltpu.VMEM((slot_count, 1, stacked), jnp.float32),
            pltpu.VMEM(by_head, jnp.bfloat16),
            pltpu.SemaphoreType.DMA((KEY_VALUE_HEADS,)),
            pltpu.SemaphoreType.DMA((count,)),
            pltpu.SemaphoreType.DMA((2,)),
            pltpu.SemaphoreType.DMA((KEY_VALUE_HEADS,)),
        ],
        compiler_params=pltpu.CompilerParams(vmem_limit_bytes=limit),
        name="merge",
    )(slots, partial, stats, slot_partial, slot_stats)


def solution(mesh):
    rows = P(("groups", "ctx"), None)
    return jax.shard_map(
        shards,
        mesh=mesh,
        in_specs=(rows, rows, rows, P(("groups", "ctx")), P(("groups", "ctx"), None, None)),
        out_specs=rows,
        check_vma=False,
    )
```
